32 devices in a mesh: occ: 8 (over z, y), vir: 4 (over x, core).
Axes of the slice: x: 2, y: 2, z: 4, core: 2. Of those that a mesh axis runs over, the one named last changes fastest.
Arguments:
- factors: bfloat16 [2, 3072, 6144], P(None, 'occ', 'vir'), may hold values from -0.41992188 to 0.41992188
- occ_energy: float32 [2], replicated, may hold values from -1.2 to -0.4
- vir_energy: float32 [3072], replicated, may hold values from 0.4 to 2.5
- block_lengths: int32 [4, 8], replicated, may hold values from 1 to 512, 1536 in all within a row
- block_owner: int32 [4, 8], replicated, may hold values from 0 to 7, each once within a row
Outputs:
- gamma_owned: bfloat16 [16384, 2, 3072], P(('occ', 'vir'))
The draws below stay inside these ranges and needn't reach their ends.
Inputs may be any that keep to these rules, and one draw needn't show every extreme that they name: `block_lengths`: each row sums to 1536, and every row's largest entry is exactly 512. `block_owner`: each row names every owner index once.
All inputs are finite; a program needn't handle non-finite values.
Results may differ from the reference program's by a relative error of at most 0.0037.
Values may be sent and summed in bfloat16 or wider, within the bound.
No kernel may reach another device: no remote copies, remote signals or barrier semaphores. Data moves between devices by JAX's collectives and lax.ppermute only.
A program may use at most 128 MiB of HBM per device.

```python
import math
import jax
import jax.numpy as jnp
import numpy as np

V = 3072
P_SIZE = 6144
OCC = 2
PQ = 1536
QUARTERS = 4
BLOCKS = 8
CAP = 512


def block_levels(rng, extent, cuts, smallest, top_value):
    factor_of = 1.0
    for axis_at, blocks in cuts:
        heights = jax.random.uniform(jax.random.fold_in(jax.random.fold_in(rng, 6), axis_at), (blocks,), jnp.float32, smallest / len(cuts), top_value / len(cuts))
        factor_of = factor_of * jnp.repeat(jnp.exp(heights), extent[axis_at] // blocks).reshape((-1,) + (1,) * (len(extent) - 1 - axis_at))
    return factor_of


def length_profile(number_of, total, reach, skew):
    loads = [(1 << 20) // math.isqrt(standing ** skew) + 1 for standing in range(2, number_of + 1)]
    surplus, given = total - reach - (number_of - 1), [1] * (number_of - 1)
    while surplus > 0:
        candidates = [i for i in range(number_of - 1) if given[i] < reach]
        pool, budget = sum([loads[i] for i in candidates]), surplus
        for i in candidates:
            more = min(reach - given[i], max(1, budget * loads[i] // pool), surplus)
            given[i] = given[i] + more
            surplus = surplus - more
    return np.array([reach] + given)


def uneven(stream_key, amount, total, limit, skew):
    if amount == 2:
        one = jax.random.randint(stream_key, (), max(1, total - limit), min(limit, total - 1) + 1)
        return jnp.stack([one, total - one])
    tallies = jnp.asarray(length_profile(amount, total, limit, skew), jnp.int32)
    pairs = (amount - 1) // 2
    donor, taker = tallies[1:1 + 2 * pairs:2], tallies[2:2 + 2 * pairs:2]
    room = jnp.minimum(donor - 1, limit - taker)
    moved = jax.random.randint(jax.random.fold_in(stream_key, 1), (pairs,), 0, 1 << 20) % (room + 1)
    tallies = tallies.at[1:1 + 2 * pairs:2].set(donor - moved).at[2:2 + 2 * pairs:2].set(taker + moved)
    return tallies[jax.random.permutation(jax.random.fold_in(stream_key, 2), amount)]


def normal_values(stream_key, dims, spread, bound, pieces=(), kind=jnp.bfloat16):
    array = spread * jax.random.normal(stream_key, dims, jnp.float32)
    if pieces:
        array = array * block_levels(stream_key, dims, pieces, -0.22, 0.18)
    return jnp.clip(array, -bound, bound).astype(kind)


def setup_inputs(seed: int = 0) -> dict:
    seeds = jax.random.split(jax.random.key(seed), 6)
    factors = normal_values(seeds[0], (OCC, V, P_SIZE), 0.07, 0.41992188, ((1, 8), (2, 4)))
    occ_energy = jnp.clip(jax.random.uniform(seeds[1], (OCC,), jnp.float32, -1.2, -0.4), -1.2, -0.4)
    vir_energy = jnp.clip(jax.random.uniform(seeds[2], (V,), jnp.float32, 0.4, 2.5), 0.4, 2.5)
    block_lengths = jax.vmap(lambda own: uneven(own, BLOCKS, PQ, CAP, 2))(jax.random.split(seeds[3], QUARTERS)).reshape((QUARTERS, BLOCKS)).astype(jnp.int32)
    block_owner = jax.vmap(lambda own: jax.random.permutation(own, BLOCKS))(jax.random.split(seeds[4], QUARTERS)).reshape((QUARTERS, BLOCKS)).astype(jnp.int32)
    return dict(factors=factors, occ_energy=occ_energy, vir_energy=vir_energy, block_lengths=block_lengths, block_owner=block_owner)


def reference(factors, occ_energy, vir_energy, block_lengths, block_owner):
    wide = factors.astype(jnp.float32)
    pair = jnp.einsum("iap,jbp->ijab", wide, wide)
    occupied_sum = occ_energy[:, None] + occ_energy[None, :]
    denominator = occupied_sum[:, :, None, None] - vir_energy[None, None, :, None] - vir_energy[None, None, None, :]
    amplitude = ((2.0 * pair - jnp.transpose(pair, (1, 0, 2, 3))) / denominator).astype(jnp.bfloat16)
    gamma = jnp.einsum("ijab,jbp->iap", amplitude.astype(jnp.float32), wide).astype(jnp.bfloat16)
    quarters = block_lengths.shape[0]
    blocks = block_lengths.shape[1]
    quarter_width = P_SIZE // quarters
    starts = (jnp.cumsum(block_lengths, axis=1) - block_lengths).astype(jnp.int32)
    owner_match = block_owner[:, None, :] == jnp.arange(blocks, dtype=jnp.int32)[None, :, None]
    dest_start = jnp.sum(jnp.where(owner_match, starts[:, None, :], 0), axis=2).astype(jnp.int32)
    dest_length = jnp.sum(jnp.where(owner_match, block_lengths[:, None, :], 0), axis=2).astype(jnp.int32)
    slot_index = jnp.arange(CAP, dtype=jnp.int32)
    offsets = jnp.arange(quarters, dtype=jnp.int32)[:, None, None] * quarter_width
    columns = offsets + jnp.minimum(dest_start[:, :, None] + slot_index[None, None, :], quarter_width - 1)
    live_slot = slot_index[None, None, :] < dest_length[:, :, None]
    columns = jnp.transpose(columns, (1, 0, 2)).reshape(-1).astype(jnp.int32)
    live_slot = jnp.transpose(live_slot, (1, 0, 2)).reshape(-1)
    picked = jnp.take(jnp.transpose(gamma, (2, 0, 1)), columns, axis=0)
    return jnp.where(live_slot[:, None, None], picked, jnp.zeros((), gamma.dtype))
```

```python
import jax
import jax.numpy as jnp
from jax import lax
from jax.sharding import PartitionSpec as P


def grid_cycle(places):
    spans = [sorted({p[d] for p in places}) for d in range(len(places[0]))]
    order = sorted(range(len(spans)), key=lambda d: -len(spans[d]))
    grid = {}
    for index, p in enumerate(places):
        grid[tuple(spans[d].index(p[d]) for d in order)] = index
    sizes = [len(spans[d]) for d in order]

    def snake(dims):
        if not dims:
            return [()]
        inner, out = snake(dims[1:]), []
        for k in range(dims[0]):
            out += [(k,) + rest for rest in (inner if k % 2 == 0 else inner[::-1])]
        return out

    rest = snake(sizes[1:])
    walk = [(k,) + rest[0] for k in range(sizes[0])]
    for back, k in enumerate(reversed(range(sizes[0]))):
        line = rest[1:]
        walk += [(k,) + r for r in (line if back % 2 == 0 else line[::-1])]
    return [grid[w] for w in walk]


def choose(marks, array):
    return lax.dot_general(marks, array, (((1,), (1,)), ((), ())), preferred_element_type=jnp.float32).astype(
        jnp.bfloat16
    )


def solution(mesh):
    cycle_size, groups = mesh.shape["occ"], mesh.shape["vir"]
    places = [tuple(row[0].coords) for row in mesh.devices.reshape(cycle_size, groups)]
    cycle = grid_cycle(places)
    position_of = [cycle.index(k) for k in range(cycle_size)]
    long_axis = max(range(3), key=lambda d: len({p[d] for p in places}))
    levels = sorted({p[long_axis] for p in places})
    planes = [[k for k in range(cycle_size) if places[k][long_axis] == level] for level in levels]
    heights, members = len(planes), len(planes[0])
    plane_of = [levels.index(p[long_axis]) for p in places]
    member_of = [planes[plane_of[k]].index(k) for k in range(cycle_size)]
    unrolled = cycle_size <= 16

    def pairs_of(target):
        return [(k * groups + v, target(k) * groups + v) for k in range(cycle_size) for v in range(groups)]

    def along_cycle(shift):
        return pairs_of(lambda k: cycle[(position_of[k] + shift) % cycle_size])

    def along_planes(shift):
        return pairs_of(lambda k: planes[(plane_of[k] + shift) % heights][member_of[k]])

    def along_members(shift):
        return pairs_of(lambda k: planes[plane_of[k]][(member_of[k] + shift) % members])

    def across_groups(bit):
        return [(k * groups + v, k * groups + (v ^ bit)) for k in range(cycle_size) for v in range(groups)]

    def send(array, pairs):
        return lax.ppermute(array, ("occ", "vir"), pairs)

    ahead, behind, core = along_cycle(1), along_cycle(-1), across_groups(1)
    wider = [across_groups(1 << bit) for bit in range(1, groups.bit_length() - 1)]

    def per_device(factors, occ_energy, vir_energy, block_lengths, block_owner):
        me, group = lax.axis_index("occ"), lax.axis_index("vir")
        occupied, tile_rows, width = factors.shape
        capacity = 8 * width // (3 * cycle_size)
        lanes = 2 if unrolled else 1
        part = tile_rows // (2 * lanes)
        even = group % 2 == 0
        occupied_sum = occ_energy[:, None] + occ_energy[None, :]

        def of_me(table):
            return lax.dynamic_index_in_dim(jnp.array(table, jnp.int32), me, 0, keepdims=False)

        def shard_at(step):
            return of_me([cycle[(position_of[k] + step) % cycle_size] for k in range(cycle_size)])

        tiles = vir_energy.reshape(cycle_size, tile_rows)
        near = lax.dynamic_index_in_dim(tiles, me, 0, keepdims=False)

        def term_of(lane, low, high, low_far, high_far):
            low_at, high_at = lane * part, (lanes + lane) * part
            mine, other = jnp.where(even, low, high), jnp.where(even, high, low)
            far = jnp.where(even, low_far[low_at : low_at + part], high_far[high_at : high_at + part])
            def pair(block):
                return jnp.einsum("iap,jbp->ijab", factors, block, preferred_element_type=jnp.float32)

            total = pair(mine) + send(pair(other), core)
            for pairs in wider:
                total = total + send(total.astype(jnp.bfloat16), pairs).astype(jnp.float32)
            denominator = (
                occupied_sum[:, :, None, None] - near[None, None, :, None] - far[None, None, None, :]
            )
            t = ((2.0 * total - jnp.transpose(total, (1, 0, 2, 3))) / denominator).astype(jnp.bfloat16)
            return [t, send(t, core)], [mine, other]

        def term(lows, highs, low_far, high_far):
            amplitude, blocks = [], []
            for lane in range(lanes):
                t, b = term_of(lane, lows[lane], highs[lane], low_far, high_far)
                amplitude, blocks = amplitude + t, blocks + b
            return jnp.einsum(
                "ijab,jbp->iap",
                jnp.concatenate(amplitude, axis=3),
                jnp.concatenate(blocks, axis=1),
                preferred_element_type=jnp.float32,
            )

        lengths = lax.dynamic_index_in_dim(block_lengths, group, 0, keepdims=False)
        owners = lax.dynamic_index_in_dim(block_owner, group, 0, keepdims=False)
        starts = jnp.cumsum(lengths) - lengths
        ordered = jnp.array([k for plane in planes for k in plane], jnp.int32)
        match = owners[None, :] == ordered[:, None]
        own_start = jnp.sum(jnp.where(match, starts[None, :], 0), axis=1)
        own_length = jnp.sum(jnp.where(match, lengths[None, :], 0), axis=1)

        lows = [factors[:, k * part : (k + 1) * part] for k in range(lanes)]
        highs = [factors[:, (lanes + k) * part : (lanes + k + 1) * part] for k in range(lanes)]
        if unrolled:
            gammas = []
            for step in range(cycle_size):
                if step >= 4:
                    lows, highs, gammas[step - 4] = lax.optimization_barrier((lows, highs, gammas[step - 4]))
                if step + 1 < cycle_size:
                    next_lows = [send(x, ahead) for x in lows]
                    next_highs = [send(x, behind) for x in highs]
                low_far = lax.dynamic_index_in_dim(tiles, shard_at(-step), 0, keepdims=False)
                high_far = lax.dynamic_index_in_dim(tiles, shard_at(step), 0, keepdims=False)
                new = term(lows, highs, low_far, high_far)
                gammas.append(new if step == 0 else gammas[-1] + new)
                lows, highs = next_lows, next_highs
            gamma = gammas[-1]
        else:
            cycle_table = jnp.array(cycle + cycle, jnp.int32)
            place = of_me(position_of)

            def one_step(step, carry):
                lows, highs, gamma = carry
                lows, highs = [send(x, ahead) for x in lows], [send(x, behind) for x in highs]
                low_far = lax.dynamic_index_in_dim(tiles, cycle_table[place + cycle_size - step], 0, keepdims=False)
                high_far = lax.dynamic_index_in_dim(tiles, cycle_table[place + step], 0, keepdims=False)
                return lows, highs, gamma + term(lows, highs, low_far, high_far)

            first = term(lows, highs, near, near)
            gamma = lax.fori_loop(1, cycle_size, one_step, (lows, highs, first))[2]
        gamma = gamma.astype(jnp.bfloat16).reshape(occupied * tile_rows, width)
        column = jnp.arange(width, dtype=jnp.int32)[None, :]
        slot = jnp.arange(capacity, dtype=jnp.int32)

        def columns_at(start, length):
            return jnp.where(slot < length, start + slot, -1)

        if not unrolled:
            wanted = jnp.where(slot[None, :] < own_length[:, None], own_start[:, None] + slot[None, :], -1)
            outgoing = choose((wanted.reshape(-1, 1) == column).astype(jnp.bfloat16), gamma)
            outgoing = outgoing.reshape(cycle_size, capacity, occupied * tile_rows)
            inverse = [ordered_at for plane in planes for ordered_at in plane]
            outgoing = jnp.stack([outgoing[inverse.index(k)] for k in range(cycle_size)])
            incoming = lax.all_to_all(outgoing, "occ", split_axis=0, concat_axis=0, tiled=True)
            incoming = incoming.reshape(cycle_size, capacity, occupied, tile_rows)
            return jnp.transpose(incoming, (1, 2, 0, 3)).reshape(capacity, occupied, cycle_size * tile_rows)

        plane_at, member_at = of_me(plane_of), of_me(member_of)
        every_match = block_owner[:, None, :] == ordered[None, :, None]
        every_length = jnp.sum(jnp.where(every_match, block_lengths[:, None, :], 0), axis=2)
        fullest = jnp.max(jnp.sum(every_length.reshape(groups, heights, members), axis=2))
        own_start, own_length = own_start.reshape(heights, members), own_length.reshape(heights, members)
        twice_start = jnp.concatenate([own_start, own_start])
        twice_length = jnp.concatenate([own_length, own_length])
        plane_start = lax.dynamic_slice_in_dim(twice_start, plane_at, heights)
        plane_length = lax.dynamic_slice_in_dim(twice_length, plane_at, heights)
        my_length = plane_length[0]
        turned = (jnp.arange(members)[:, None] + member_at) % members == jnp.arange(members)[None, :]
        turned_length = jnp.sum(jnp.where(turned, my_length[None, :], 0), axis=1)
        turned_offset = jnp.sum(jnp.where(turned, (jnp.cumsum(my_length) - my_length)[None, :], 0), axis=1)
        turned_start = jnp.sum(jnp.where(turned, plane_start[0][None, :], 0), axis=1)

        def exchange(room):
            def run(gamma):
                wide = jnp.arange(room, dtype=jnp.int32)
                wide_column = wide[None, :]
                result = jnp.zeros((capacity, occupied, cycle_size * tile_rows), jnp.bfloat16)
                for rise in range(heights):
                    if rise:
                        wanted = jnp.full((room,), -1, jnp.int32)
                        at = jnp.zeros((), jnp.int32)
                        for m in range(members):
                            length = plane_length[rise, m]
                            here = (wide >= at) & (wide < at + length)
                            wanted = jnp.where(here, plane_start[rise, m] + wide - at, wanted)
                            at = at + length
                        packed = choose((wanted[:, None] == column).astype(jnp.bfloat16), gamma)
                        packed = send(packed, along_planes(rise))
                    for turn in range(members):
                        if rise:
                            wanted = jnp.where(slot < turned_length[turn], turned_offset[turn] + slot, -1)
                            marks = (wanted[:, None] == wide_column).astype(jnp.bfloat16)
                            piece = jnp.dot(marks, packed, preferred_element_type=jnp.float32).astype(jnp.bfloat16)
                        else:
                            wanted = columns_at(turned_start[turn], turned_length[turn])
                            piece = choose((wanted[:, None] == column).astype(jnp.bfloat16), gamma)
                        if turn:
                            piece = send(piece, along_members(turn))
                        source = of_me(
                            [
                                planes[(plane_of[k] - rise) % heights][(member_of[k] - turn) % members]
                                for k in range(cycle_size)
                            ]
                        )
                        piece = piece.reshape(capacity, occupied, tile_rows)
                        result = lax.dynamic_update_slice_in_dim(result, piece, source * tile_rows, 2)
                return result

            return run

        rooms = list(range(capacity, members * capacity + 1, capacity // 8))
        which = jnp.sum((fullest > jnp.array(rooms, jnp.int32)).astype(jnp.int32))
        return lax.switch(which, [exchange(room) for room in rooms], gamma)

    placed = (P(None, "occ", "vir"), P(), P(), P(), P())
    return jax.shard_map(
        per_device,
        mesh=mesh,
        in_specs=placed,
        out_specs=P(("occ", "vir"), None, None),
        check_vma=False,
    )
```

```python
import functools

import jax
import jax.numpy as jnp
from jax import lax
from jax.experimental import pallas as pl
from jax.experimental.pallas import tpu as pltpu
from jax.sharding import PartitionSpec as P

def grid_cycle(places):
    spans = [sorted({p[d] for p in places}) for d in range(len(places[0]))]
    order = sorted(range(len(spans)), key=lambda d: -len(spans[d]))
    grid = {}
    for index, p in enumerate(places):
        grid[tuple(spans[d].index(p[d]) for d in order)] = index
    sizes = [len(spans[d]) for d in order]

    def snake(dims):
        if not dims:
            return [()]
        inner, out = snake(dims[1:]), []
        for k in range(dims[0]):
            out += [(k,) + rest for rest in (inner if k % 2 == 0 else inner[::-1])]
        return out

    rest = snake(sizes[1:])
    walk = [(k,) + rest[0] for k in range(sizes[0])]
    for back, k in enumerate(reversed(range(sizes[0]))):
        line = rest[1:]
        walk += [(k,) + r for r in (line if back % 2 == 0 else line[::-1])]
    return [grid[w] for w in walk]


def steps_of(rows):
    return 2 if rows % 32 == 0 else 1


def pack_kernel(rise, table_ref, gamma_ref, out_ref):
    rows, width = out_ref.shape[0], gamma_ref.shape[1]
    slot = pl.program_id(0) * rows + lax.broadcasted_iota(jnp.int32, (rows, width), 0)
    column = lax.broadcasted_iota(jnp.int32, (rows, width), 1)
    first, count = table_ref[rise, 0], table_ref[rise, 1]
    second, more = table_ref[rise, 2], table_ref[rise, 3]
    wanted = jnp.where(slot < count, first + slot, second + slot - count)
    marks = jnp.where((column == wanted) & (slot < count + more), 1.0, 0.0).astype(jnp.bfloat16)
    picked = lax.dot_general(marks, gamma_ref[...], (((1,), (1,)), ((), ())), preferred_element_type=jnp.float32)
    out_ref[...] = picked.astype(jnp.bfloat16)


def pack(table, gamma, rise, room):
    rows, width = gamma.shape
    steps = steps_of(room)
    return pl.pallas_call(
        functools.partial(pack_kernel, rise),
        grid_spec=pltpu.PrefetchScalarGridSpec(
            num_scalar_prefetch=1,
            grid=(steps,),
            in_specs=[pl.BlockSpec((rows, width), lambda g, table: (0, 0))],
            out_specs=pl.BlockSpec((room // steps, rows), lambda g, table: (g, 0)),
        ),
        out_shape=jax.ShapeDtypeStruct((room, rows), jnp.bfloat16),
        compiler_params=pltpu.CompilerParams(vmem_limit_bytes=40 << 20),
        cost_estimate=pl.CostEstimate(
            flops=2 * room * rows * width, bytes_accessed=2 * rows * (width + room), transcendentals=0
        ),
    )(table, gamma)


def place_kernel(at, table_ref, packed_ref, *refs):
    out_ref = refs[-1]
    rows, room = out_ref.shape[0], packed_ref.shape[0]
    slot = pl.program_id(0) * rows + lax.broadcasted_iota(jnp.int32, (rows, room), 0)
    column = lax.broadcasted_iota(jnp.int32, (rows, room), 1)
    hit = (column == slot + table_ref[at, 1]) & (slot < table_ref[at, 2])
    marks = jnp.where(hit, 1.0, 0.0).astype(jnp.bfloat16)
    picked = jnp.dot(marks, packed_ref[...], preferred_element_type=jnp.float32).astype(jnp.bfloat16)
    tile_rows = out_ref.shape[2]
    for i in range(out_ref.shape[1]):
        out_ref[:, i, :] = picked[:, i * tile_rows : (i + 1) * tile_rows]


def place(table, packed, result, at, shape, tile_rows):
    room, rows = packed.shape
    steps = steps_of(shape[0])
    whole = [] if result is None else [result]
    return pl.pallas_call(
        functools.partial(place_kernel, at),
        grid_spec=pltpu.PrefetchScalarGridSpec(
            num_scalar_prefetch=1,
            grid=(steps,),
            in_specs=[pl.BlockSpec((room, rows), lambda g, table: (0, 0))] + [pl.BlockSpec(memory_space=pl.ANY)] * len(whole),
            out_specs=pl.BlockSpec((shape[0] // steps, shape[1], tile_rows), lambda g, table: (g, 0, table[at, 0])),
        ),
        out_shape=jax.ShapeDtypeStruct(shape, jnp.bfloat16),
        input_output_aliases={2: 0} if whole else {},
        compiler_params=pltpu.CompilerParams(vmem_limit_bytes=40 << 20),
        cost_estimate=pl.CostEstimate(
            flops=2 * shape[0] * rows * room, bytes_accessed=2 * rows * (shape[0] + room), transcendentals=0
        ),
    )(table, packed, *whole)


def setup_kernel(rooms, turns, at_ref, order_ref, lengths_ref, owners_ref, energy_ref, *outs):
    down_ref, up_ref, near_ref, pack_ref, place_ref, which_ref = outs
    me, group = at_ref[0], at_ref[1]
    cycle_size = energy_ref.shape[0]
    heights = turns // 2
    groups, blocks = lengths_ref.shape
    near_ref[...] = energy_ref[pl.ds(me, 1), :]
    for step in range(cycle_size):
        down_ref[pl.ds(step, 1), :] = energy_ref[pl.ds(order_ref[me, step], 1), :]
        up_ref[pl.ds(step, 1), :] = energy_ref[pl.ds(order_ref[me, cycle_size + step], 1), :]
    targets, sources, levels = 2 * cycle_size, 2 * cycle_size + turns, 2 * cycle_size + 2 * turns
    found = []
    for turn in range(turns):
        owner = order_ref[me, targets + turn]
        start, length, so_far = jnp.int32(0), jnp.int32(0), jnp.int32(0)
        for k in range(blocks):
            hit = owners_ref[group, k] == owner
            start = jnp.where(hit, so_far, start)
            length = jnp.where(hit, lengths_ref[group, k], length)
            so_far = so_far + lengths_ref[group, k]
        pack_ref[turn // 2, 2 * (turn % 2)] = start
        pack_ref[turn // 2, 2 * (turn % 2) + 1] = length
        found.append(length)
    for turn in range(turns):
        place_ref[turn, 0] = order_ref[me, sources + turn]
        place_ref[turn, 1] = found[0] if turn % 2 == 0 else jnp.int32(0)
        place_ref[turn, 2] = found[1]
    fullest = jnp.int32(0)
    for g in range(groups):
        held = [jnp.int32(0)] * heights
        for k in range(blocks):
            level = order_ref[owners_ref[g, k], levels]
            held = [h + jnp.where(level == at, lengths_ref[g, k], 0) for at, h in enumerate(held)]
        for h in held:
            fullest = jnp.maximum(fullest, h)
    which = jnp.int32(0)
    for room in rooms:
        which = which + jnp.where(fullest > room, 1, 0)
    which_ref[0] = which


def setup(at, order, lengths, owners, energy, rooms, turns):
    scalars, vectors = pl.BlockSpec(memory_space=pltpu.SMEM), pl.BlockSpec(memory_space=pltpu.VMEM)
    return pl.pallas_call(
        functools.partial(setup_kernel, rooms, turns),
        in_specs=[scalars] * 4 + [vectors],
        out_specs=[vectors] * 3 + [scalars] * 3,
        out_shape=[
            jax.ShapeDtypeStruct(energy.shape, jnp.float32),
            jax.ShapeDtypeStruct(energy.shape, jnp.float32),
            jax.ShapeDtypeStruct((1, energy.shape[1]), jnp.float32),
            jax.ShapeDtypeStruct((turns // 2, 4), jnp.int32),
            jax.ShapeDtypeStruct((turns, 3), jnp.int32),
            jax.ShapeDtypeStruct((1,), jnp.int32),
        ],
    )(at, order, lengths, owners, energy)


def solution(mesh):
    cycle_size, groups = mesh.shape["occ"], mesh.shape["vir"]
    places = [tuple(row[0].coords) for row in mesh.devices.reshape(cycle_size, groups)]
    cycle = grid_cycle(places)
    position_of = [cycle.index(k) for k in range(cycle_size)]
    long_axis = max(range(3), key=lambda d: len({p[d] for p in places}))
    levels = sorted({p[long_axis] for p in places})
    planes = [[k for k in range(cycle_size) if places[k][long_axis] == level] for level in levels]
    heights, members = len(planes), len(planes[0])
    plane_of = [levels.index(p[long_axis]) for p in places]
    member_of = [planes[plane_of[k]].index(k) for k in range(cycle_size)]
    in_pairs = cycle_size <= 16 and members == 2

    def pairs_of(target):
        return [(k * groups + v, target(k, v) * groups + v) for k in range(cycle_size) for v in range(groups)]

    def along_planes(shift):
        return pairs_of(lambda k, v: planes[(plane_of[k] + shift) % heights][member_of[k]])

    def across_groups(bit):
        return [(k * groups + v, k * groups + (v ^ bit)) for k in range(cycle_size) for v in range(groups)]

    def send(array, pairs):
        return lax.ppermute(array, ("occ", "vir"), pairs)

    onward = pairs_of(lambda k, v: cycle[(position_of[k] + (1 if v % 2 == 0 else -1)) % cycle_size])
    partner = pairs_of(lambda k, v: planes[plane_of[k]][(member_of[k] + 1) % members])
    core = across_groups(1)
    wider = [across_groups(1 << bit) for bit in range(1, groups.bit_length() - 1)]

    def per_device(factors, occ_energy, vir_energy, block_lengths, block_owner):
        me, group = lax.axis_index("occ"), lax.axis_index("vir")
        occupied, tile_rows, width = factors.shape
        capacity = 8 * width // (3 * cycle_size)
        half = tile_rows // 2
        even = group % 2 == 0

        def of_me(table):
            return lax.dynamic_index_in_dim(
                jnp.array(table, jnp.int32), me, 0, keepdims=False, allow_negative_indices=False
            )

        low, high = factors[:, :half], factors[:, half:]
        near_mine, apart_mine = jnp.where(even, low, high), jnp.where(even, high, low)
        mine, other = near_mine, send(apart_mine, core)
        rows_mine, rows_other = mine, other

        tiles = vir_energy.reshape(cycle_size, tile_rows)
        if in_pairs:
            order = [
                [cycle[position_of[k] - step] for step in range(cycle_size)]
                + [cycle[(position_of[k] + step) % cycle_size] for step in range(cycle_size)]
                + [
                    planes[(plane_of[k] + rise) % heights][(member_of[k] + 1 - turn) % members]
                    for rise in range(heights)
                    for turn in range(members)
                ]
                + [
                    planes[(plane_of[k] - rise) % heights][(member_of[k] + turn) % members]
                    for rise in range(heights)
                    for turn in range(members)
                ]
                + [plane_of[k]]
                for k in range(cycle_size)
            ]
            rooms = list(range(capacity, members * capacity + 1, capacity // 8))
            other, tiles = lax.optimization_barrier((other, tiles))
            at = jnp.stack([me, group]).astype(jnp.int32)
            order = jnp.array(order, jnp.int32)
            down, up, own, pack_table, place_table, which = setup(
                at, order, block_lengths, block_owner, tiles, rooms, heights * members
            )
            own = own[0]
        else:
            in_cycle = jnp.stack([tiles[k] for k in cycle + cycle])
            up = lax.dynamic_slice_in_dim(in_cycle, of_me(position_of), cycle_size, allow_negative_indices=False)
            down = jnp.stack([up[-k] for k in range(cycle_size)])
            own = lax.dynamic_index_in_dim(tiles, me, 0, keepdims=False, allow_negative_indices=False)
        far_low, far_high = down[:, :half], up[:, half:]
        far = jnp.where(
            even, jnp.concatenate([far_low, far_high], 1), jnp.concatenate([far_high, far_low], 1)
        )
        near = jnp.where(even, own[:half], own[half:])
        base = (occ_energy[:, None] + occ_energy[None, :])[:, :, None, None] - near[None, None, :, None]

        def pair(first, second):
            one = jnp.einsum("iap,jbp->ijab", rows_mine, first, preferred_element_type=jnp.float32)
            return one + jnp.einsum("iap,jbp->ijab", rows_other, second, preferred_element_type=jnp.float32)

        def sums_of(mine, other, their_mine, their_other):
            return jnp.concatenate([pair(mine, other), pair(their_other, their_mine)], axis=3)

        def term(total, mine, other, their_mine, their_other, far):
            for pairs in wider:
                total = total + send(total.astype(jnp.bfloat16), pairs).astype(jnp.float32)
            swapped = jnp.transpose(total, (1, 0, 2, 3))
            t = ((2.0 * total - swapped) / (base - far[None, None, None, :])).astype(jnp.bfloat16)

            def product(ring, core):
                return jnp.einsum(
                    "ijab,jbp->iap", t, jnp.concatenate([ring, core], 1), preferred_element_type=jnp.float32
                )

            return product(mine, their_other), product(other, their_mine)

        def swap(mine, other):
            return send(mine, core), send(other, core)

        if in_pairs:
            sums, totals = [], []
            for step in range(cycle_size):
                if step >= 2:
                    mine, totals[step - 1] = lax.optimization_barrier((mine, totals[step - 1]))
                if step >= 4:
                    other, sums[step - 3] = lax.optimization_barrier((other, sums[step - 3]))
                if step + 1 < cycle_size:
                    next_mine, next_other = send(mine, onward), send(other, onward)
                theirs = swap(mine, other) if step else (send(near_mine, core), apart_mine)
                totals.append(sums_of(mine, other, *theirs))
                new = term(totals[-1], mine, other, *theirs, far[step])
                sums.append(new if step == 0 else (sums[-1][0] + new[0], sums[-1][1] + new[1]))
                mine, other = next_mine, next_other
            sum_mine, sum_other = sums[-1]
        else:

            def one_step(step, carry):
                mine, other, sum_mine, sum_other = carry
                mine, other = send(mine, onward), send(other, onward)
                theirs = swap(mine, other)
                new = term(
                    sums_of(mine, other, *theirs),
                    mine,
                    other,
                    *theirs,
                    lax.dynamic_index_in_dim(far, step, 0, keepdims=False),
                )
                return mine, other, sum_mine + new[0], sum_other + new[1]

            theirs = swap(mine, other)
            first = term(sums_of(mine, other, *theirs), mine, other, *theirs, far[0])
            sum_mine, sum_other = lax.fori_loop(1, cycle_size, one_step, (mine, other, *first))[2:]
        near_gamma, apart_gamma = sum_mine.astype(jnp.bfloat16), send(sum_other.astype(jnp.bfloat16), core)
        gamma = jnp.concatenate(
            [jnp.where(even, near_gamma, apart_gamma), jnp.where(even, apart_gamma, near_gamma)], axis=1
        ).reshape(occupied * tile_rows, width)

        if not in_pairs:
            lengths = lax.dynamic_index_in_dim(block_lengths, group, 0, keepdims=False)
            owners = lax.dynamic_index_in_dim(block_owner, group, 0, keepdims=False)
            starts = jnp.cumsum(lengths) - lengths
            match = owners[None, :] == jnp.arange(cycle_size, dtype=jnp.int32)[:, None]
            to_start = jnp.sum(jnp.where(match, starts[None, :], 0), axis=1)
            to_length = jnp.sum(jnp.where(match, lengths[None, :], 0), axis=1)
            slot = jnp.arange(capacity, dtype=jnp.int32)
            column = jnp.arange(width, dtype=jnp.int32)
            wanted = jnp.where(slot[None, :] < to_length[:, None], to_start[:, None] + slot[None, :], -1)
            marks = (wanted.reshape(-1, 1) == column[None, :]).astype(jnp.bfloat16)
            outgoing = jnp.einsum("sp,rp->sr", marks, gamma, preferred_element_type=jnp.float32)
            outgoing = outgoing.astype(jnp.bfloat16).reshape(cycle_size, capacity, occupied * tile_rows)
            incoming = lax.all_to_all(outgoing, "occ", split_axis=0, concat_axis=0, tiled=True)
            incoming = incoming.reshape(cycle_size, capacity, occupied, tile_rows)
            return jnp.transpose(incoming, (1, 2, 0, 3)).reshape(capacity, occupied, cycle_size * tile_rows)

        shape = (capacity, occupied, cycle_size * tile_rows)

        def exchange(room, gamma, pack_table, place_table):
            packed = []
            for rise in list(range(1, heights)) + [0]:
                piece = pack(pack_table, gamma, rise, room)
                packed.append((rise, send(piece, along_planes(rise)) if rise else piece))
            result = None
            for rise, piece in packed[-1:] + packed[:-1]:
                mine = piece[:capacity]
                if result is not None:
                    mine, result = lax.optimization_barrier((mine, result))
                theirs = send(mine, partner)
                result = place(place_table, piece, result, rise * members, shape, tile_rows)
                if rise != heights - 1:
                    result = place(place_table, theirs, result, rise * members + 1, shape, tile_rows)
            result = place(place_table, theirs, result, rise * members + 1, shape, tile_rows)
            return result

        return lax.switch(
            which[0], [functools.partial(exchange, room) for room in rooms], gamma, pack_table, place_table
        )

    placed = (P(None, "occ", "vir"), P(), P(), P(), P())
    return jax.shard_map(
        per_device,
        mesh=mesh,
        in_specs=placed,
        out_specs=P(("occ", "vir"), None, None),
        check_vma=False,
    )
```

```python
import functools
import math

import jax
import jax.numpy as jnp
from jax import lax
from jax.experimental import pallas as pl
from jax.experimental.pallas import tpu as pltpu
from jax.sharding import PartitionSpec as P

def grid_cycle(places):
    spans = [sorted({p[d] for p in places}) for d in range(len(places[0]))]
    order = sorted(range(len(spans)), key=lambda d: -len(spans[d]))
    grid = {}
    for index, p in enumerate(places):
        grid[tuple(spans[d].index(p[d]) for d in order)] = index
    sizes = [len(spans[d]) for d in order]

    def snake(dims):
        if not dims:
            return [()]
        inner, out = snake(dims[1:]), []
        for k in range(dims[0]):
            out += [(k,) + rest for rest in (inner if k % 2 == 0 else inner[::-1])]
        return out

    rest = snake(sizes[1:])
    walk = [(k,) + rest[0] for k in range(sizes[0])]
    for back, k in enumerate(reversed(range(sizes[0]))):
        line = rest[1:]
        walk += [(k,) + r for r in (line if back % 2 == 0 else line[::-1])]
    return [grid[w] for w in walk]


def pack_kernel(rise, base, table_ref, gamma_ref, out_ref):
    slots, occupied, tile_rows = out_ref.shape
    width = gamma_ref.shape[1]
    slot = base + pl.program_id(0) * slots + lax.broadcasted_iota(jnp.int32, (slots, width), 0)
    column = lax.broadcasted_iota(jnp.int32, (slots, width), 1)
    first, count = table_ref[rise, 0], table_ref[rise, 1]
    second, more = table_ref[rise, 2], table_ref[rise, 3]
    wanted = jnp.where(slot < count, first + slot, second + slot - count)
    marks = jnp.where((column == wanted) & (slot < count + more), 1.0, 0.0).astype(jnp.bfloat16)
    picked = lax.dot_general(marks, gamma_ref[...], (((1,), (1,)), ((), ())), preferred_element_type=jnp.float32)
    for i in range(occupied):
        out_ref[:, i, :] = picked[:, i * tile_rows : (i + 1) * tile_rows].astype(jnp.bfloat16)


def pack(table, gamma, rise, base, room, occupied):
    rows, width = gamma.shape
    steps = 2 if room % 32 == 0 and room > 256 else 1
    return pl.pallas_call(
        functools.partial(pack_kernel, rise, base),
        grid_spec=pltpu.PrefetchScalarGridSpec(
            num_scalar_prefetch=1,
            grid=(steps,),
            in_specs=[pl.BlockSpec((rows, width), lambda g, table: (0, 0))],
            out_specs=pl.BlockSpec((room // steps, occupied, rows // occupied), lambda g, table: (g, 0, 0)),
        ),
        out_shape=jax.ShapeDtypeStruct((room, occupied, rows // occupied), jnp.bfloat16),
        compiler_params=pltpu.CompilerParams(vmem_limit_bytes=40 << 20),
        cost_estimate=pl.CostEstimate(
            flops=2 * room * rows * width, bytes_accessed=2 * rows * (width + room), transcendentals=0
        ),
    )(table, gamma)


def place_kernel(at, parts, table_ref, *refs):
    out_ref, joined_ref = refs[-2], refs[-1]
    slots = out_ref.shape[0]
    offset, length = table_ref[at, 1], table_ref[at, 2]
    source = refs[0]
    if parts > 1:
        so_far = 0
        for ref in refs[:parts]:
            joined_ref[pl.ds(so_far, ref.shape[0])] = ref[...]
            so_far += ref.shape[0]
        source = joined_ref
    few = math.gcd(slots, 32)

    @pl.loop(0, slots // few)
    def _(k):
        slot = k * few + lax.broadcasted_iota(jnp.int32, (few,) + out_ref.shape[1:], 0)
        start = k * few + (offset if parts > 1 else 0)
        block = source[pl.ds(start, few)].astype(jnp.float32)
        out_ref[pl.ds(k * few, few)] = jnp.where(slot < length, block, 0.0).astype(jnp.bfloat16)


def place(table, pieces, result, at, shape, tile_rows):
    slots, occupied = shape[0], shape[1]
    whole = [] if result is None else [result]
    return pl.pallas_call(
        functools.partial(place_kernel, at, len(pieces)),
        grid_spec=pltpu.PrefetchScalarGridSpec(
            num_scalar_prefetch=1,
            grid=(1,),
            in_specs=[pl.BlockSpec(x.shape, lambda g, table: (0, 0, 0)) for x in pieces]
            + [pl.BlockSpec(memory_space=pl.ANY)] * len(whole),
            out_specs=pl.BlockSpec((slots, occupied, tile_rows), lambda g, table: (0, 0, table[at, 0])),
            scratch_shapes=[pltpu.VMEM((2 * slots if len(pieces) > 1 else 8, occupied, tile_rows), jnp.bfloat16)],
        ),
        out_shape=jax.ShapeDtypeStruct(shape, jnp.bfloat16),
        input_output_aliases={1 + len(pieces): 0} if whole else {},
        compiler_params=pltpu.CompilerParams(vmem_limit_bytes=40 << 20),
        cost_estimate=pl.CostEstimate(
            flops=slots * occupied * tile_rows,
            bytes_accessed=6 * slots * occupied * tile_rows,
            transcendentals=0,
        ),
    )(table, *pieces, *whole)


def setup_kernel(rooms, turns, at_ref, order_ref, lengths_ref, owners_ref, energy_ref, *outs):
    down_ref, up_ref, near_ref, pack_ref, place_ref, which_ref = outs
    me, group = at_ref[0], at_ref[1]
    cycle_size = energy_ref.shape[0]
    heights = turns // 2
    groups, blocks = lengths_ref.shape
    near_ref[...] = energy_ref[pl.ds(me, 1), :]
    for step in range(cycle_size):
        down_ref[pl.ds(step, 1), :] = energy_ref[pl.ds(order_ref[me, step], 1), :]
        up_ref[pl.ds(step, 1), :] = energy_ref[pl.ds(order_ref[me, cycle_size + step], 1), :]
    targets, sources, levels = 2 * cycle_size, 2 * cycle_size + turns, 2 * cycle_size + 2 * turns
    found = []
    for turn in range(turns):
        owner = order_ref[me, targets + turn]
        start, length, so_far = jnp.int32(0), jnp.int32(0), jnp.int32(0)
        for k in range(blocks):
            hit = owners_ref[group, k] == owner
            start = jnp.where(hit, so_far, start)
            length = jnp.where(hit, lengths_ref[group, k], length)
            so_far = so_far + lengths_ref[group, k]
        pack_ref[turn // 2, 2 * (turn % 2)] = start
        pack_ref[turn // 2, 2 * (turn % 2) + 1] = length
        found.append(length)
    for turn in range(turns):
        place_ref[turn, 0] = order_ref[me, sources + turn]
        place_ref[turn, 1] = found[0] if turn % 2 == 0 else jnp.int32(0)
        place_ref[turn, 2] = found[1]
    fullest = jnp.int32(0)
    for g in range(groups):
        held = [jnp.int32(0)] * heights
        for k in range(blocks):
            level = order_ref[owners_ref[g, k], levels]
            held = [h + jnp.where(level == at, lengths_ref[g, k], 0) for at, h in enumerate(held)]
        for h in held:
            fullest = jnp.maximum(fullest, h)
    which = jnp.int32(0)
    for room in rooms:
        which = which + jnp.where(fullest > room, 1, 0)
    which_ref[0] = which


def setup(at, order, lengths, owners, energy, rooms, turns):
    scalars, vectors = pl.BlockSpec(memory_space=pltpu.SMEM), pl.BlockSpec(memory_space=pltpu.VMEM)
    return pl.pallas_call(
        functools.partial(setup_kernel, rooms, turns),
        in_specs=[scalars] * 4 + [vectors],
        out_specs=[vectors] * 3 + [scalars] * 3,
        out_shape=[
            jax.ShapeDtypeStruct(energy.shape, jnp.float32),
            jax.ShapeDtypeStruct(energy.shape, jnp.float32),
            jax.ShapeDtypeStruct((1, energy.shape[1]), jnp.float32),
            jax.ShapeDtypeStruct((turns // 2, 4), jnp.int32),
            jax.ShapeDtypeStruct((turns, 3), jnp.int32),
            jax.ShapeDtypeStruct((1,), jnp.int32),
        ],
    )(at, order, lengths, owners, energy)


def solution(mesh):
    cycle_size, groups = mesh.shape["occ"], mesh.shape["vir"]
    places = [tuple(row[0].coords) for row in mesh.devices.reshape(cycle_size, groups)]
    cycle = grid_cycle(places)
    position_of = [cycle.index(k) for k in range(cycle_size)]
    long_axis = max(range(3), key=lambda d: len({p[d] for p in places}))
    levels = sorted({p[long_axis] for p in places})
    planes = [[k for k in range(cycle_size) if places[k][long_axis] == level] for level in levels]
    heights, members = len(planes), len(planes[0])
    plane_of = [levels.index(p[long_axis]) for p in places]
    member_of = [planes[plane_of[k]].index(k) for k in range(cycle_size)]
    in_pairs = cycle_size <= 16 and members == 2

    def pairs_of(target):
        return [(k * groups + v, target(k, v) * groups + v) for k in range(cycle_size) for v in range(groups)]

    def along_planes(shift):
        return pairs_of(lambda k, v: planes[(plane_of[k] + shift) % heights][member_of[k]])

    def across_groups(bit):
        return [(k * groups + v, k * groups + (v ^ bit)) for k in range(cycle_size) for v in range(groups)]

    def send(array, pairs):
        return lax.ppermute(array, ("occ", "vir"), pairs)

    onward = pairs_of(lambda k, v: cycle[(position_of[k] + (1 if v % 2 == 0 else -1)) % cycle_size])
    partner = pairs_of(lambda k, v: planes[plane_of[k]][(member_of[k] + 1) % members])
    core = across_groups(1)
    wider = [across_groups(1 << bit) for bit in range(1, groups.bit_length() - 1)]

    def per_device(factors, occ_energy, vir_energy, block_lengths, block_owner):
        me, group = lax.axis_index("occ"), lax.axis_index("vir")
        occupied, tile_rows, width = factors.shape
        capacity = 8 * width // (3 * cycle_size)
        half = tile_rows // 2
        even = group % 2 == 0

        def of_me(table):
            return lax.dynamic_index_in_dim(
                jnp.array(table, jnp.int32), me, 0, keepdims=False, allow_negative_indices=False
            )

        low, high = factors[:, :half], factors[:, half:]
        near_mine, apart_mine = jnp.where(even, low, high), jnp.where(even, high, low)
        mine, other = near_mine, send(apart_mine, core)
        rows_mine, rows_other = mine, other

        tiles = vir_energy.reshape(cycle_size, tile_rows)
        if in_pairs:
            order = [
                [cycle[position_of[k] - step] for step in range(cycle_size)]
                + [cycle[(position_of[k] + step) % cycle_size] for step in range(cycle_size)]
                + [
                    planes[(plane_of[k] + rise) % heights][(member_of[k] + 1 - turn) % members]
                    for rise in range(heights)
                    for turn in range(members)
                ]
                + [
                    planes[(plane_of[k] - rise) % heights][(member_of[k] + turn) % members]
                    for rise in range(heights)
                    for turn in range(members)
                ]
                + [plane_of[k]]
                for k in range(cycle_size)
            ]
            rooms = list(range(capacity, members * capacity + 1, capacity // 8))
            other, tiles = lax.optimization_barrier((other, tiles))
            at = jnp.stack([me, group]).astype(jnp.int32)
            order = jnp.array(order, jnp.int32)
            down, up, own, pack_table, place_table, which = setup(
                at, order, block_lengths, block_owner, tiles, rooms, heights * members
            )
            own = own[0]
        else:
            in_cycle = jnp.stack([tiles[k] for k in cycle + cycle])
            up = lax.dynamic_slice_in_dim(in_cycle, of_me(position_of), cycle_size, allow_negative_indices=False)
            down = jnp.stack([up[-k] for k in range(cycle_size)])
            own = lax.dynamic_index_in_dim(tiles, me, 0, keepdims=False, allow_negative_indices=False)
        far_low, far_high = down[:, :half], up[:, half:]
        far = jnp.where(
            even, jnp.concatenate([far_low, far_high], 1), jnp.concatenate([far_high, far_low], 1)
        )
        near = jnp.where(even, own[:half], own[half:])
        base = (occ_energy[:, None] + occ_energy[None, :])[:, :, None, None] - near[None, None, :, None]

        def pair(first, second):
            one = jnp.einsum("iap,jbp->ijab", rows_mine, first, preferred_element_type=jnp.float32)
            return one + jnp.einsum("iap,jbp->ijab", rows_other, second, preferred_element_type=jnp.float32)

        def sums_of(mine, other, their_mine, their_other):
            return jnp.concatenate([pair(mine, other), pair(their_other, their_mine)], axis=3)

        def across(total):
            for pairs in wider:
                total = total + send(total.astype(jnp.bfloat16), pairs).astype(jnp.float32)
            return total

        def term(total, mine, other, their_mine, their_other, far):
            swapped = jnp.transpose(total, (1, 0, 2, 3))
            t = ((2.0 * total - swapped) / (base - far[None, None, None, :])).astype(jnp.bfloat16)

            def product(ring, core):
                return jnp.einsum(
                    "ijab,jbp->iap", t, jnp.concatenate([ring, core], 1), preferred_element_type=jnp.float32
                )

            return product(mine, their_other), product(other, their_mine)

        def swap(mine, other):
            return send(mine, core), send(other, core)

        if in_pairs:
            sums, totals, sent = [], [], []
            for step in range(cycle_size):
                if step == cycle_size - 1:
                    mine, sent[step - 1] = lax.optimization_barrier((mine, sent[step - 1]))
                elif step >= 2:
                    mine, totals[step - 1] = lax.optimization_barrier((mine, totals[step - 1]))
                if step >= 4:
                    other, sums[step - 3] = lax.optimization_barrier((other, sums[step - 3]))
                if step + 1 < cycle_size:
                    next_mine, next_other = send(mine, onward), send(other, onward)
                theirs = swap(mine, other) if step else (send(near_mine, core), apart_mine)
                totals.append([pair(mine, other), pair(theirs[1], theirs[0])])
                if step < cycle_size - 1:
                    sent.append(across(jnp.concatenate(totals[-1], axis=3)))
                else:
                    sent.append(jnp.concatenate([across(total) for total in totals[-1]], axis=3))
                new = term(sent[-1], mine, other, *theirs, far[step])
                sums.append(new if step == 0 else (sums[-1][0] + new[0], sums[-1][1] + new[1]))
                mine, other = next_mine, next_other
            sum_mine, sum_other = sums[-1]
        else:

            def one_step(step, carry):
                mine, other, sum_mine, sum_other = carry
                mine, other = send(mine, onward), send(other, onward)
                theirs = swap(mine, other)
                new = term(
                    across(sums_of(mine, other, *theirs)),
                    mine,
                    other,
                    *theirs,
                    lax.dynamic_index_in_dim(far, step, 0, keepdims=False),
                )
                return mine, other, sum_mine + new[0], sum_other + new[1]

            theirs = swap(mine, other)
            first = term(across(sums_of(mine, other, *theirs)), mine, other, *theirs, far[0])
            sum_mine, sum_other = lax.fori_loop(1, cycle_size, one_step, (mine, other, *first))[2:]
        near_gamma, apart_gamma = sum_mine.astype(jnp.bfloat16), send(sum_other.astype(jnp.bfloat16), core)
        gamma = jnp.concatenate(
            [jnp.where(even, near_gamma, apart_gamma), jnp.where(even, apart_gamma, near_gamma)], axis=1
        ).reshape(occupied * tile_rows, width)

        if not in_pairs:
            lengths = lax.dynamic_index_in_dim(block_lengths, group, 0, keepdims=False)
            owners = lax.dynamic_index_in_dim(block_owner, group, 0, keepdims=False)
            starts = jnp.cumsum(lengths) - lengths
            match = owners[None, :] == jnp.arange(cycle_size, dtype=jnp.int32)[:, None]
            to_start = jnp.sum(jnp.where(match, starts[None, :], 0), axis=1)
            to_length = jnp.sum(jnp.where(match, lengths[None, :], 0), axis=1)
            slot = jnp.arange(capacity, dtype=jnp.int32)
            column = jnp.arange(width, dtype=jnp.int32)
            wanted = jnp.where(slot[None, :] < to_length[:, None], to_start[:, None] + slot[None, :], -1)
            marks = (wanted.reshape(-1, 1) == column[None, :]).astype(jnp.bfloat16)
            outgoing = jnp.einsum("sp,rp->sr", marks, gamma, preferred_element_type=jnp.float32)
            outgoing = outgoing.astype(jnp.bfloat16).reshape(cycle_size, capacity, occupied * tile_rows)
            incoming = lax.all_to_all(outgoing, "occ", split_axis=0, concat_axis=0, tiled=True)
            incoming = incoming.reshape(cycle_size, capacity, occupied, tile_rows)
            return jnp.transpose(incoming, (1, 2, 0, 3)).reshape(capacity, occupied, cycle_size * tile_rows)

        shape = (capacity, occupied, cycle_size * tile_rows)

        def after(array, other):
            return lax.optimization_barrier((array, other))[0]

        rises = sorted(range(1, heights), key=lambda rise: min(rise, heights - rise))
        landed = {}
        for at, rise in enumerate(rises):
            piece = pack(pack_table, gamma, rise, 0, capacity, occupied)
            if at >= 2:
                piece = after(piece, landed[rises[at - 2]])
            landed[rise] = send(piece, along_planes(rise))
        landed[0] = pack(pack_table, gamma, 0, 0, capacity, occupied)
        theirs = {rise: send(landed[rise], partner) for rise in [0] + rises[:-1]}
        result = place(place_table, [theirs[0]], None, 1, shape, tile_rows)
        result = place(place_table, [theirs[rises[0]]], result, rises[0] * members + 1, shape, tile_rows)

        def rest(room, gamma, pack_table, place_table, landed, result):
            pieces = {rise: [landed[rise]] for rise in landed}
            for rise in (rises + [0]) * (room > 0):
                piece = pack(pack_table, gamma, rise, capacity, room, occupied)
                pieces[rise].append(send(piece, along_planes(rise)) if rise else piece)
            last = send(landed[rises[-1]], partner)
            for rise in [0] + rises:
                mine = pieces[rise] if room else [landed[rise], landed[rise][:8]]
                result = place(place_table, mine, result, rise * members, shape, tile_rows)
            return place(place_table, [last], result, rises[-1] * members + 1, shape, tile_rows)

        rests = [functools.partial(rest, room - capacity) for room in rooms]
        result = lax.switch(which[0], rests, gamma, pack_table, place_table, landed, result)
        for rise in rises[1:-1]:
            result = place(place_table, [theirs[rise]], result, rise * members + 1, shape, tile_rows)
        return result

    placed = (P(None, "occ", "vir"), P(), P(), P(), P())
    return jax.shard_map(
        per_device,
        mesh=mesh,
        in_specs=placed,
        out_specs=P(("occ", "vir"), None, None),
        check_vma=False,
    )
```

```python
import functools
import math

import jax
import jax.numpy as jnp
from jax import lax
from jax.experimental import pallas as pl
from jax.experimental.pallas import tpu as pltpu
from jax.sharding import PartitionSpec as P

def grid_cycle(places):
    spans = [sorted({p[d] for p in places}) for d in range(len(places[0]))]
    order = sorted(range(len(spans)), key=lambda d: -len(spans[d]))
    grid = {}
    for index, p in enumerate(places):
        grid[tuple(spans[d].index(p[d]) for d in order)] = index
    sizes = [len(spans[d]) for d in order]

    def snake(dims):
        if not dims:
            return [()]
        inner, out = snake(dims[1:]), []
        for k in range(dims[0]):
            out += [(k,) + rest for rest in (inner if k % 2 == 0 else inner[::-1])]
        return out

    rest = snake(sizes[1:])
    walk = [(k,) + rest[0] for k in range(sizes[0])]
    for back, k in enumerate(reversed(range(sizes[0]))):
        line = rest[1:]
        walk += [(k,) + r for r in (line if back % 2 == 0 else line[::-1])]
    return [grid[w] for w in walk]


def pack_kernel(rise, base, table_ref, gamma_ref, out_ref):
    slots, occupied, tile_rows = out_ref.shape
    width = gamma_ref.shape[1]
    slot = base + pl.program_id(0) * slots + lax.broadcasted_iota(jnp.int32, (slots, width), 0)
    column = lax.broadcasted_iota(jnp.int32, (slots, width), 1)
    first, count = table_ref[rise, 0], table_ref[rise, 1]
    second, more = table_ref[rise, 2], table_ref[rise, 3]
    wanted = jnp.where(slot < count, first + slot, second + slot - count)
    marks = jnp.where((column == wanted) & (slot < count + more), 1.0, 0.0).astype(jnp.bfloat16)
    picked = lax.dot_general(marks, gamma_ref[...], (((1,), (1,)), ((), ())), preferred_element_type=jnp.float32)
    for i in range(occupied):
        out_ref[:, i, :] = picked[:, i * tile_rows : (i + 1) * tile_rows].astype(jnp.bfloat16)


def pack(table, gamma, rise, base, room, occupied):
    rows, width = gamma.shape
    steps = 2 if room % 32 == 0 and room > 256 else 1
    return pl.pallas_call(
        functools.partial(pack_kernel, rise, base),
        grid_spec=pltpu.PrefetchScalarGridSpec(
            num_scalar_prefetch=1,
            grid=(steps,),
            in_specs=[pl.BlockSpec((rows, width), lambda g, table: (0, 0))],
            out_specs=pl.BlockSpec((room // steps, occupied, rows // occupied), lambda g, table: (g, 0, 0)),
        ),
        out_shape=jax.ShapeDtypeStruct((room, occupied, rows // occupied), jnp.bfloat16),
        compiler_params=pltpu.CompilerParams(vmem_limit_bytes=40 << 20),
        cost_estimate=pl.CostEstimate(
            flops=2 * room * rows * width, bytes_accessed=2 * rows * (width + room), transcendentals=0
        ),
    )(table, gamma)


def place_kernel(at, parts, table_ref, *refs):
    out_ref, seam_ref = refs[-2], refs[-1]
    slots = out_ref.shape[0]
    offset, length = table_ref[at, 1], table_ref[at, 2]
    few = seam_ref.shape[0] // 4
    first_ref, more_ref = refs[0], refs[parts - 1]
    end = slots + more_ref.shape[0] - few
    if parts > 1:
        seam_ref[pl.ds(0, few)] = first_ref[pl.ds(slots - few, few)]
        seam_ref[pl.ds(few, few)] = more_ref[pl.ds(0, few)]
        seam_ref[pl.ds(2 * few, few)] = more_ref[pl.ds(more_ref.shape[0] - few, few)]

    def fill(k, source, start):
        slot = k * few + lax.broadcasted_iota(jnp.int32, (few,) + out_ref.shape[1:], 0)
        block = source[pl.ds(start, few)].astype(jnp.float32)
        out_ref[pl.ds(k * few, few)] = jnp.where(slot < length, block, 0.0).astype(jnp.bfloat16)

    @pl.loop(0, slots // few)
    def _(k):
        if parts == 1:
            fill(k, first_ref, k * few)
            return
        start = offset + k * few
        last = slots - few

        @pl.when(start <= last)
        def _():
            fill(k, first_ref, start)

        @pl.when((start > last) & (start < slots))
        def _():
            fill(k, seam_ref, start - last)

        @pl.when((start >= slots) & (start <= end))
        def _():
            fill(k, more_ref, start - slots)

        @pl.when((start >= slots) & (start > end))
        def _():
            fill(k, seam_ref, 2 * few + jnp.minimum(start - end, few))


def place(table, pieces, result, at, shape, tile_rows):
    slots, occupied = shape[0], shape[1]
    whole = [] if result is None else [result]
    return pl.pallas_call(
        functools.partial(place_kernel, at, len(pieces)),
        grid_spec=pltpu.PrefetchScalarGridSpec(
            num_scalar_prefetch=1,
            grid=(1,),
            in_specs=[pl.BlockSpec(x.shape, lambda g, table: (0, 0, 0)) for x in pieces]
            + [pl.BlockSpec(memory_space=pl.ANY)] * len(whole),
            out_specs=pl.BlockSpec((slots, occupied, tile_rows), lambda g, table: (0, 0, table[at, 0])),
            scratch_shapes=[pltpu.VMEM((4 * math.gcd(slots, 32), occupied, tile_rows), jnp.bfloat16)],
        ),
        out_shape=jax.ShapeDtypeStruct(shape, jnp.bfloat16),
        input_output_aliases={1 + len(pieces): 0} if whole else {},
        compiler_params=pltpu.CompilerParams(vmem_limit_bytes=40 << 20),
        cost_estimate=pl.CostEstimate(
            flops=slots * occupied * tile_rows,
            bytes_accessed=6 * slots * occupied * tile_rows,
            transcendentals=0,
        ),
    )(table, *pieces, *whole)


def setup_kernel(rooms, turns, at_ref, order_ref, lengths_ref, owners_ref, energy_ref, *outs):
    down_ref, up_ref, near_ref, pack_ref, place_ref, which_ref = outs
    me, group = at_ref[0], at_ref[1]
    cycle_size = energy_ref.shape[0]
    heights = turns // 2
    groups, blocks = lengths_ref.shape
    near_ref[...] = energy_ref[pl.ds(me, 1), :]
    for step in range(cycle_size):
        down_ref[pl.ds(step, 1), :] = energy_ref[pl.ds(order_ref[me, step], 1), :]
        up_ref[pl.ds(step, 1), :] = energy_ref[pl.ds(order_ref[me, cycle_size + step], 1), :]
    targets, sources, levels = 2 * cycle_size, 2 * cycle_size + turns, 2 * cycle_size + 2 * turns
    found = []
    for turn in range(turns):
        owner = order_ref[me, targets + turn]
        start, length, so_far = jnp.int32(0), jnp.int32(0), jnp.int32(0)
        for k in range(blocks):
            hit = owners_ref[group, k] == owner
            start = jnp.where(hit, so_far, start)
            length = jnp.where(hit, lengths_ref[group, k], length)
            so_far = so_far + lengths_ref[group, k]
        pack_ref[turn // 2, 2 * (turn % 2)] = start
        pack_ref[turn // 2, 2 * (turn % 2) + 1] = length
        found.append(length)
    for turn in range(turns):
        place_ref[turn, 0] = order_ref[me, sources + turn]
        place_ref[turn, 1] = found[0] if turn % 2 == 0 else jnp.int32(0)
        place_ref[turn, 2] = found[1]
    fullest = jnp.int32(0)
    for g in range(groups):
        held = [jnp.int32(0)] * heights
        for k in range(blocks):
            level = order_ref[owners_ref[g, k], levels]
            held = [h + jnp.where(level == at, lengths_ref[g, k], 0) for at, h in enumerate(held)]
        for h in held:
            fullest = jnp.maximum(fullest, h)
    which = jnp.int32(0)
    for room in rooms:
        which = which + jnp.where(fullest > room, 1, 0)
    which_ref[0] = which


def setup(at, order, lengths, owners, energy, rooms, turns):
    scalars, vectors = pl.BlockSpec(memory_space=pltpu.SMEM), pl.BlockSpec(memory_space=pltpu.VMEM)
    return pl.pallas_call(
        functools.partial(setup_kernel, rooms, turns),
        in_specs=[scalars] * 4 + [vectors],
        out_specs=[vectors] * 3 + [scalars] * 3,
        out_shape=[
            jax.ShapeDtypeStruct(energy.shape, jnp.float32),
            jax.ShapeDtypeStruct(energy.shape, jnp.float32),
            jax.ShapeDtypeStruct((1, energy.shape[1]), jnp.float32),
            jax.ShapeDtypeStruct((turns // 2, 4), jnp.int32),
            jax.ShapeDtypeStruct((turns, 3), jnp.int32),
            jax.ShapeDtypeStruct((1,), jnp.int32),
        ],
    )(at, order, lengths, owners, energy)


def solution(mesh):
    cycle_size, groups = mesh.shape["occ"], mesh.shape["vir"]
    places = [tuple(row[0].coords) for row in mesh.devices.reshape(cycle_size, groups)]
    cycle = grid_cycle(places)
    position_of = [cycle.index(k) for k in range(cycle_size)]
    long_axis = max(range(3), key=lambda d: len({p[d] for p in places}))
    levels = sorted({p[long_axis] for p in places})
    planes = [[k for k in range(cycle_size) if places[k][long_axis] == level] for level in levels]
    heights, members = len(planes), len(planes[0])
    plane_of = [levels.index(p[long_axis]) for p in places]
    member_of = [planes[plane_of[k]].index(k) for k in range(cycle_size)]
    in_pairs = cycle_size <= 16 and members == 2

    def pairs_of(target):
        return [(k * groups + v, target(k, v) * groups + v) for k in range(cycle_size) for v in range(groups)]

    def along_planes(shift):
        return pairs_of(lambda k, v: planes[(plane_of[k] + shift) % heights][member_of[k]])

    def across_groups(bit):
        return [(k * groups + v, k * groups + (v ^ bit)) for k in range(cycle_size) for v in range(groups)]

    def send(array, pairs):
        return lax.ppermute(array, ("occ", "vir"), pairs)

    onward = pairs_of(lambda k, v: cycle[(position_of[k] + (1 if v % 2 == 0 else -1)) % cycle_size])
    partner = pairs_of(lambda k, v: planes[plane_of[k]][(member_of[k] + 1) % members])
    core = across_groups(1)
    wider = [across_groups(1 << bit) for bit in range(1, groups.bit_length() - 1)]

    def per_device(factors, occ_energy, vir_energy, block_lengths, block_owner):
        me, group = lax.axis_index("occ"), lax.axis_index("vir")
        occupied, tile_rows, width = factors.shape
        capacity = 8 * width // (3 * cycle_size)
        half = tile_rows // 2
        even = group % 2 == 0

        def of_me(table):
            return lax.dynamic_index_in_dim(
                jnp.array(table, jnp.int32), me, 0, keepdims=False, allow_negative_indices=False
            )

        low, high = factors[:, :half], factors[:, half:]
        near_mine, apart_mine = jnp.where(even, low, high), jnp.where(even, high, low)
        mine, other = near_mine, send(apart_mine, core)
        rows_mine, rows_other = mine, other

        tiles = vir_energy.reshape(cycle_size, tile_rows)
        if in_pairs:
            order = [
                [cycle[position_of[k] - step] for step in range(cycle_size)]
                + [cycle[(position_of[k] + step) % cycle_size] for step in range(cycle_size)]
                + [
                    planes[(plane_of[k] + rise) % heights][(member_of[k] + 1 - turn) % members]
                    for rise in range(heights)
                    for turn in range(members)
                ]
                + [
                    planes[(plane_of[k] - rise) % heights][(member_of[k] + turn) % members]
                    for rise in range(heights)
                    for turn in range(members)
                ]
                + [plane_of[k]]
                for k in range(cycle_size)
            ]
            rooms = list(range(capacity, members * capacity + 1, capacity // 8))
            other, tiles = lax.optimization_barrier((other, tiles))
            at = jnp.stack([me, group]).astype(jnp.int32)
            order = jnp.array(order, jnp.int32)
            down, up, own, pack_table, place_table, which = setup(
                at, order, block_lengths, block_owner, tiles, rooms, heights * members
            )
            own = own[0]
        else:
            in_cycle = jnp.stack([tiles[k] for k in cycle + cycle])
            up = lax.dynamic_slice_in_dim(in_cycle, of_me(position_of), cycle_size, allow_negative_indices=False)
            down = jnp.stack([up[-k] for k in range(cycle_size)])
            own = lax.dynamic_index_in_dim(tiles, me, 0, keepdims=False, allow_negative_indices=False)
        far_low, far_high = down[:, :half], up[:, half:]
        far = jnp.where(
            even, jnp.concatenate([far_low, far_high], 1), jnp.concatenate([far_high, far_low], 1)
        )
        near = jnp.where(even, own[:half], own[half:])
        base = (occ_energy[:, None] + occ_energy[None, :])[:, :, None, None] - near[None, None, :, None]

        def pair(first, second):
            one = jnp.einsum("iap,jbp->ijab", rows_mine, first, preferred_element_type=jnp.float32)
            return one + jnp.einsum("iap,jbp->ijab", rows_other, second, preferred_element_type=jnp.float32)

        def sums_of(mine, other, their_mine, their_other):
            return jnp.concatenate([pair(mine, other), pair(their_other, their_mine)], axis=3)

        def across(total):
            for pairs in wider:
                total = total + send(total.astype(jnp.bfloat16), pairs).astype(jnp.float32)
            return total

        def term(total, mine, other, their_mine, their_other, far):
            swapped = jnp.transpose(total, (1, 0, 2, 3))
            t = ((2.0 * total - swapped) / (base - far[None, None, None, :])).astype(jnp.bfloat16)

            def product(ring, core):
                return jnp.einsum(
                    "ijab,jbp->iap", t, jnp.concatenate([ring, core], 1), preferred_element_type=jnp.float32
                )

            return product(mine, their_other), product(other, their_mine)

        def swap(mine, other):
            return send(mine, core), send(other, core)

        if in_pairs:
            sums, totals, sent = [], [], []
            for step in range(cycle_size):
                if step >= 2:
                    mine, totals[step - 1], sent[step - 2] = lax.optimization_barrier((mine, totals[step - 1], sent[step - 2]))
                if step >= 4:
                    other, sums[step - 3] = lax.optimization_barrier((other, sums[step - 3]))
                if step + 1 < cycle_size:
                    next_mine, next_other = send(mine, onward), send(other, onward)
                theirs = swap(mine, other) if step else (send(near_mine, core), apart_mine)
                totals.append(pair(jnp.concatenate([mine, theirs[1]], 1), jnp.concatenate([other, theirs[0]], 1)))
                if step >= 1:
                    totals[step], sent[step - 1] = lax.optimization_barrier((totals[step], sent[step - 1]))
                sent.append(across(totals[-1]))
                new = term(sent[-1], mine, other, *theirs, far[step])
                sums.append(new if step == 0 else (sums[-1][0] + new[0], sums[-1][1] + new[1]))
                mine, other = next_mine, next_other
            sum_mine, sum_other = sums[-1]
        else:

            def one_step(step, carry):
                mine, other, sum_mine, sum_other = carry
                mine, other = send(mine, onward), send(other, onward)
                theirs = swap(mine, other)
                new = term(
                    across(sums_of(mine, other, *theirs)),
                    mine,
                    other,
                    *theirs,
                    lax.dynamic_index_in_dim(far, step, 0, keepdims=False),
                )
                return mine, other, sum_mine + new[0], sum_other + new[1]

            theirs = swap(mine, other)
            first = term(across(sums_of(mine, other, *theirs)), mine, other, *theirs, far[0])
            sum_mine, sum_other = lax.fori_loop(1, cycle_size, one_step, (mine, other, *first))[2:]
        near_gamma, apart_gamma = sum_mine.astype(jnp.bfloat16), send(sum_other.astype(jnp.bfloat16), core)
        gamma = jnp.concatenate(
            [jnp.where(even, near_gamma, apart_gamma), jnp.where(even, apart_gamma, near_gamma)], axis=1
        ).reshape(occupied * tile_rows, width)

        if not in_pairs:
            lengths = lax.dynamic_index_in_dim(block_lengths, group, 0, keepdims=False)
            owners = lax.dynamic_index_in_dim(block_owner, group, 0, keepdims=False)
            starts = jnp.cumsum(lengths) - lengths
            match = owners[None, :] == jnp.arange(cycle_size, dtype=jnp.int32)[:, None]
            to_start = jnp.sum(jnp.where(match, starts[None, :], 0), axis=1)
            to_length = jnp.sum(jnp.where(match, lengths[None, :], 0), axis=1)
            slot = jnp.arange(capacity, dtype=jnp.int32)
            column = jnp.arange(width, dtype=jnp.int32)
            wanted = jnp.where(slot[None, :] < to_length[:, None], to_start[:, None] + slot[None, :], -1)
            marks = (wanted.reshape(-1, 1) == column[None, :]).astype(jnp.bfloat16)
            outgoing = jnp.einsum("sp,rp->sr", marks, gamma, preferred_element_type=jnp.float32)
            outgoing = outgoing.astype(jnp.bfloat16).reshape(cycle_size, capacity, occupied * tile_rows)
            incoming = lax.all_to_all(outgoing, "occ", split_axis=0, concat_axis=0, tiled=True)
            incoming = incoming.reshape(cycle_size, capacity, occupied, tile_rows)
            return jnp.transpose(incoming, (1, 2, 0, 3)).reshape(capacity, occupied, cycle_size * tile_rows)

        shape = (capacity, occupied, cycle_size * tile_rows)

        def after(array, other):
            return lax.optimization_barrier((array, other))[0]

        rises = sorted(range(1, heights), key=lambda rise: min(rise, heights - rise))
        landed = {}
        for at, rise in enumerate(rises):
            piece = pack(pack_table, gamma, rise, 0, capacity, occupied)
            if at >= 2:
                piece = after(piece, landed[rises[at - 2]])
            landed[rise] = send(piece, along_planes(rise))
        landed[0] = pack(pack_table, gamma, 0, 0, capacity, occupied)
        theirs = {rise: send(landed[rise], partner) for rise in [0] + rises[:-1]}
        more = {rise: pack(pack_table, gamma, rise, capacity, rooms[-1] - capacity, occupied) for rise in rises + [0]}
        result = None
        for rise in [0] + rises[:-1]:
            result = place(place_table, [theirs[rise]], result, rise * members + 1, shape, tile_rows)

        def rest(room, more, place_table, landed, result):
            room = max(room, 32)
            pieces = {rise: [landed[rise], send(more[rise][:room], along_planes(rise))] for rise in rises}
            pieces[0] = [landed[0], more[0]]
            last = send(landed[rises[-1]], partner)
            for rise in [0] + rises[:-1]:
                result = place(place_table, pieces[rise], result, rise * members, shape, tile_rows)
            result = place(place_table, [last], result, rises[-1] * members + 1, shape, tile_rows)
            return place(place_table, pieces[rises[-1]], result, rises[-1] * members, shape, tile_rows)

        rests = [functools.partial(rest, room - capacity) for room in rooms]
        return lax.switch(which[0], rests, more, place_table, landed, result)

    placed = (P(None, "occ", "vir"), P(), P(), P(), P())
    return jax.shard_map(
        per_device,
        mesh=mesh,
        in_specs=placed,
        out_specs=P(("occ", "vir"), None, None),
        check_vma=False,
    )
```

```python
import functools
import math

import jax
import jax.numpy as jnp
from jax import lax
from jax.experimental import pallas as pl
from jax.experimental.pallas import tpu as pltpu
from jax.sharding import PartitionSpec as P

def grid_cycle(places):
    spans = [sorted({p[d] for p in places}) for d in range(len(places[0]))]
    order = sorted(range(len(spans)), key=lambda d: -len(spans[d]))
    grid = {}
    for index, p in enumerate(places):
        grid[tuple(spans[d].index(p[d]) for d in order)] = index
    sizes = [len(spans[d]) for d in order]

    def snake(dims):
        if not dims:
            return [()]
        inner, out = snake(dims[1:]), []
        for k in range(dims[0]):
            out += [(k,) + rest for rest in (inner if k % 2 == 0 else inner[::-1])]
        return out

    rest = snake(sizes[1:])
    walk = [(k,) + rest[0] for k in range(sizes[0])]
    for back, k in enumerate(reversed(range(sizes[0]))):
        line = rest[1:]
        walk += [(k,) + r for r in (line if back % 2 == 0 else line[::-1])]
    return [grid[w] for w in walk]


def pack_kernel(rise, base, table_ref, gamma_ref, out_ref):
    slots, occupied, tile_rows = out_ref.shape
    width = gamma_ref.shape[1]
    slot = base + pl.program_id(0) * slots + lax.broadcasted_iota(jnp.int32, (slots, width), 0)
    column = lax.broadcasted_iota(jnp.int32, (slots, width), 1)
    first, count = table_ref[rise, 0], table_ref[rise, 1]
    second, more = table_ref[rise, 2], table_ref[rise, 3]
    wanted = jnp.where(slot < count, first + slot, second + slot - count)
    marks = jnp.where((column == wanted) & (slot < count + more), 1.0, 0.0).astype(jnp.bfloat16)
    picked = lax.dot_general(marks, gamma_ref[...], (((1,), (1,)), ((), ())), preferred_element_type=jnp.float32)
    for i in range(occupied):
        out_ref[:, i, :] = picked[:, i * tile_rows : (i + 1) * tile_rows].astype(jnp.bfloat16)


def pack(table, gamma, rise, base, room, occupied):
    rows, width = gamma.shape
    steps = 2 if room % 32 == 0 and room > 256 else 1
    return pl.pallas_call(
        functools.partial(pack_kernel, rise, base),
        grid_spec=pltpu.PrefetchScalarGridSpec(
            num_scalar_prefetch=1,
            grid=(steps,),
            in_specs=[pl.BlockSpec((rows, width), lambda g, table: (0, 0))],
            out_specs=pl.BlockSpec((room // steps, occupied, rows // occupied), lambda g, table: (g, 0, 0)),
        ),
        out_shape=jax.ShapeDtypeStruct((room, occupied, rows // occupied), jnp.bfloat16),
        compiler_params=pltpu.CompilerParams(vmem_limit_bytes=40 << 20),
        cost_estimate=pl.CostEstimate(
            flops=2 * room * rows * width, bytes_accessed=2 * rows * (width + room), transcendentals=0
        ),
    )(table, gamma)


def copy_slots(out_ref, at, source_ref):
    few = math.gcd(source_ref.shape[0], 32)

    @pl.loop(0, source_ref.shape[0] // few)
    def _(k):
        out_ref[pl.ds(at + k * few, few)] = source_ref[pl.ds(k * few, few)]


def join_kernel(rise, table_ref, mine_ref, theirs_ref, out_ref):
    first = table_ref[rise, 0]

    @pl.when(table_ref[rise, 1] == 0)
    def _():
        copy_slots(out_ref, 0, mine_ref)
        copy_slots(out_ref, first, theirs_ref)

    @pl.when(table_ref[rise, 1] != 0)
    def _():
        copy_slots(out_ref, 0, theirs_ref)
        copy_slots(out_ref, first, mine_ref)


def join(table, mine, theirs, rise):
    slots, occupied, tile_rows = mine.shape
    return pl.pallas_call(
        functools.partial(join_kernel, rise),
        in_specs=[pl.BlockSpec(memory_space=pltpu.SMEM)] + [pl.BlockSpec(memory_space=pltpu.VMEM)] * 2,
        out_specs=pl.BlockSpec(memory_space=pltpu.VMEM),
        out_shape=jax.ShapeDtypeStruct((2 * slots, occupied, tile_rows), jnp.bfloat16),
        compiler_params=pltpu.CompilerParams(vmem_limit_bytes=40 << 20),
        cost_estimate=pl.CostEstimate(
            flops=slots, bytes_accessed=8 * slots * occupied * tile_rows, transcendentals=0
        ),
    )(table, mine, theirs)


def place_kernel(at, parts, table_ref, *refs):
    out_ref, seam_ref, later_ref = refs[-3:]
    slots = out_ref.shape[0]
    offset, length, skip, odd = [table_ref[at, k] for k in range(1, 5)]
    few = seam_ref.shape[0] // 2
    first_ref = refs[0]
    if parts == 2:
        copy_slots(later_ref, 0, refs[1])
    if parts == 3:
        lane = refs[1].shape[0]

        @pl.when(odd == 0)
        def _():
            copy_slots(later_ref, 0, refs[1])
            copy_slots(later_ref, lane, refs[2])

        @pl.when(odd != 0)
        def _():
            copy_slots(later_ref, 0, refs[2])
            copy_slots(later_ref, lane, refs[1])

    if parts > 1:
        seam_ref[pl.ds(0, few)] = first_ref[pl.ds(slots - few, few)]
        seam_ref[pl.ds(few, few)] = later_ref[pl.ds(skip, few)]

    def fill(k, source, start):
        @pl.when((k + 1) * few <= length)
        def _():
            out_ref[pl.ds(k * few, few)] = source[pl.ds(start, few)]

        @pl.when((k + 1) * few > length)
        def _():
            slot = k * few + lax.broadcasted_iota(jnp.int32, (few,) + out_ref.shape[1:], 0)
            block = source[pl.ds(start, few)].astype(jnp.float32)
            out_ref[pl.ds(k * few, few)] = jnp.where(slot < length, block, 0.0).astype(jnp.bfloat16)

    def some(k):
        if parts == 1:
            fill(k, first_ref, k * few)
            return
        start = offset + k * few
        last = slots - few

        @pl.when(start <= last)
        def _():
            fill(k, first_ref, start)

        @pl.when((start > last) & (start < slots))
        def _():
            fill(k, seam_ref, start - last)

        @pl.when(start >= slots)
        def _():
            fill(k, later_ref, skip + start - slots)

    @pl.loop(0, slots // few)
    def _(k):
        @pl.when(k * few >= length)
        def _():
            out_ref[pl.ds(k * few, few)] = jnp.zeros((few,) + out_ref.shape[1:], jnp.bfloat16)

        @pl.when(k * few < length)
        def _():
            some(k)


def place(table, pieces, result, at, shape, tile_rows):
    slots, occupied = shape[0], shape[1]
    whole = [] if result is None else [result]
    return pl.pallas_call(
        functools.partial(place_kernel, at, len(pieces)),
        grid_spec=pltpu.PrefetchScalarGridSpec(
            num_scalar_prefetch=1,
            grid=(1,),
            in_specs=[pl.BlockSpec(x.shape, lambda g, table: (0, 0, 0)) for x in pieces]
            + [pl.BlockSpec(memory_space=pl.ANY)] * len(whole),
            out_specs=pl.BlockSpec((slots, occupied, tile_rows), lambda g, table: (0, 0, table[at, 0])),
            scratch_shapes=[
                pltpu.VMEM((2 * math.gcd(slots, 32), occupied, tile_rows), jnp.bfloat16),
                pltpu.VMEM((2 * slots + 64 if len(pieces) > 1 else 8, occupied, tile_rows), jnp.bfloat16),
            ],
        ),
        out_shape=jax.ShapeDtypeStruct(shape, jnp.bfloat16),
        input_output_aliases={1 + len(pieces): 0} if whole else {},
        compiler_params=pltpu.CompilerParams(vmem_limit_bytes=40 << 20),
        cost_estimate=pl.CostEstimate(
            flops=slots * occupied * tile_rows,
            bytes_accessed=6 * slots * occupied * tile_rows,
            transcendentals=0,
        ),
    )(table, *pieces, *whole)


def setup_kernel(rooms, capacity, turns, at_ref, order_ref, lengths_ref, owners_ref, energy_ref, *outs):
    down_ref, up_ref, near_ref, pack_ref, place_ref, join_ref, which_ref = outs
    me, group = at_ref[0], at_ref[1]
    cycle_size = energy_ref.shape[0]
    heights = turns // 2
    groups, blocks = lengths_ref.shape
    near_ref[...] = energy_ref[pl.ds(me, 1), :]
    for step in range(cycle_size):
        down_ref[pl.ds(step, 1), :] = energy_ref[pl.ds(order_ref[me, step], 1), :]
        up_ref[pl.ds(step, 1), :] = energy_ref[pl.ds(order_ref[me, cycle_size + step], 1), :]
    targets, sources, levels = 2 * cycle_size, 2 * cycle_size + turns, 2 * cycle_size + 2 * turns
    found = []
    for turn in range(turns):
        owner = order_ref[me, targets + turn]
        start, length, so_far = jnp.int32(0), jnp.int32(0), jnp.int32(0)
        for k in range(blocks):
            hit = owners_ref[group, k] == owner
            start = jnp.where(hit, so_far, start)
            length = jnp.where(hit, lengths_ref[group, k], length)
            so_far = so_far + lengths_ref[group, k]
        pack_ref[turn // 2, 2 * (turn % 2)] = start
        pack_ref[turn // 2, 2 * (turn % 2) + 1] = length
        found.append(length)
    later = []
    for g in range(groups):
        held = [jnp.int32(0)] * heights
        for k in range(blocks):
            level = order_ref[owners_ref[g, k], levels]
            held = [h + jnp.where(level == at, lengths_ref[g, k], 0) for at, h in enumerate(held)]
        later.append([jnp.maximum(h - capacity, 0) for h in held])
    need = jnp.int32(0)
    for g in range(0, groups, 2):
        for one, two in zip(later[g], later[g + 1]):
            need = jnp.maximum(need, (one + two + 1) // 2)
    odd = group % 2
    my_level = order_ref[me, levels]
    for rise in range(heights):
        evens = jnp.int32(0)
        for g in range(0, groups, 2):
            for level in range(heights):
                here = (group - odd == g) & ((my_level + rise) % heights == level)
                evens = jnp.where(here, later[g][level], evens)
        join_ref[rise, 0] = evens
        join_ref[rise, 1] = odd
        if rise == 0:
            skip = jnp.where(odd == 0, 0, evens)
    for turn in range(turns):
        place_ref[turn, 0] = order_ref[me, sources + turn]
        place_ref[turn, 1] = found[0] if turn % 2 == 0 else jnp.int32(0)
        place_ref[turn, 2] = found[1]
        place_ref[turn, 3] = skip if turn >= 2 else jnp.int32(0)
        place_ref[turn, 4] = odd
    which = jnp.int32(0)
    for room in rooms[:-1]:
        which = which + jnp.where(need > room, 1, 0)
    which_ref[0] = which


def setup(at, order, lengths, owners, energy, rooms, capacity, turns):
    scalars, vectors = pl.BlockSpec(memory_space=pltpu.SMEM), pl.BlockSpec(memory_space=pltpu.VMEM)
    return pl.pallas_call(
        functools.partial(setup_kernel, rooms, capacity, turns),
        in_specs=[scalars] * 4 + [vectors],
        out_specs=[vectors] * 3 + [scalars] * 4,
        out_shape=[
            jax.ShapeDtypeStruct(energy.shape, jnp.float32),
            jax.ShapeDtypeStruct(energy.shape, jnp.float32),
            jax.ShapeDtypeStruct((1, energy.shape[1]), jnp.float32),
            jax.ShapeDtypeStruct((turns // 2, 4), jnp.int32),
            jax.ShapeDtypeStruct((turns, 5), jnp.int32),
            jax.ShapeDtypeStruct((turns // 2, 2), jnp.int32),
            jax.ShapeDtypeStruct((1,), jnp.int32),
        ],
    )(at, order, lengths, owners, energy)


def solution(mesh):
    cycle_size, groups = mesh.shape["occ"], mesh.shape["vir"]
    places = [tuple(row[0].coords) for row in mesh.devices.reshape(cycle_size, groups)]
    cycle = grid_cycle(places)
    position_of = [cycle.index(k) for k in range(cycle_size)]
    long_axis = max(range(3), key=lambda d: len({p[d] for p in places}))
    levels = sorted({p[long_axis] for p in places})
    planes = [[k for k in range(cycle_size) if places[k][long_axis] == level] for level in levels]
    heights, members = len(planes), len(planes[0])
    plane_of = [levels.index(p[long_axis]) for p in places]
    member_of = [planes[plane_of[k]].index(k) for k in range(cycle_size)]
    in_pairs = cycle_size <= 16 and members == 2

    def pairs_of(target):
        return [(k * groups + v, target(k, v) * groups + v) for k in range(cycle_size) for v in range(groups)]

    def along_planes(shift):
        return pairs_of(lambda k, v: planes[(plane_of[k] + shift) % heights][member_of[k]])

    def across_groups(bit):
        return [(k * groups + v, k * groups + (v ^ bit)) for k in range(cycle_size) for v in range(groups)]

    def send(array, pairs):
        return lax.ppermute(array, ("occ", "vir"), pairs)

    onward = pairs_of(lambda k, v: cycle[(position_of[k] + (1 if v % 2 == 0 else -1)) % cycle_size])
    partner = pairs_of(lambda k, v: planes[plane_of[k]][(member_of[k] + 1) % members])
    core = across_groups(1)
    wider = [across_groups(1 << bit) for bit in range(1, groups.bit_length() - 1)]

    def per_device(factors, occ_energy, vir_energy, block_lengths, block_owner):
        me, group = lax.axis_index("occ"), lax.axis_index("vir")
        occupied, tile_rows, width = factors.shape
        capacity = 8 * width // (3 * cycle_size)
        half = tile_rows // 2
        even = group % 2 == 0

        def of_me(table):
            return lax.dynamic_index_in_dim(
                jnp.array(table, jnp.int32), me, 0, keepdims=False, allow_negative_indices=False
            )

        low, high = factors[:, :half], factors[:, half:]
        near_mine, apart_mine = jnp.where(even, low, high), jnp.where(even, high, low)
        mine, other = near_mine, send(apart_mine, core)
        rows_mine, rows_other = mine, other

        tiles = vir_energy.reshape(cycle_size, tile_rows)
        if in_pairs:
            order = [
                [cycle[position_of[k] - step] for step in range(cycle_size)]
                + [cycle[(position_of[k] + step) % cycle_size] for step in range(cycle_size)]
                + [
                    planes[(plane_of[k] + rise) % heights][(member_of[k] + 1 - turn) % members]
                    for rise in range(heights)
                    for turn in range(members)
                ]
                + [
                    planes[(plane_of[k] - rise) % heights][(member_of[k] + turn) % members]
                    for rise in range(heights)
                    for turn in range(members)
                ]
                + [plane_of[k]]
                for k in range(cycle_size)
            ]
            grain = capacity // 16
            rooms = [grain * k for k in (1, 2, 3, 4, 5, 6, 7, 8, 10, 12, 14, 16)]
            other, tiles = lax.optimization_barrier((other, tiles))
            at = jnp.stack([me, group]).astype(jnp.int32)
            order = jnp.array(order, jnp.int32)
            down, up, own, pack_table, place_table, join_table, which = setup(
                at, order, block_lengths, block_owner, tiles, rooms, capacity, heights * members
            )
            own = own[0]
        else:
            in_cycle = jnp.stack([tiles[k] for k in cycle + cycle])
            up = lax.dynamic_slice_in_dim(in_cycle, of_me(position_of), cycle_size, allow_negative_indices=False)
            down = jnp.stack([up[-k] for k in range(cycle_size)])
            own = lax.dynamic_index_in_dim(tiles, me, 0, keepdims=False, allow_negative_indices=False)
        far_low, far_high = down[:, :half], up[:, half:]
        far = jnp.where(
            even, jnp.concatenate([far_low, far_high], 1), jnp.concatenate([far_high, far_low], 1)
        )
        near = jnp.where(even, own[:half], own[half:])
        base = (occ_energy[:, None] + occ_energy[None, :])[:, :, None, None] - near[None, None, :, None]

        def pair(first, second):
            one = jnp.einsum("iap,jbp->ijab", rows_mine, first, preferred_element_type=jnp.float32)
            return one + jnp.einsum("iap,jbp->ijab", rows_other, second, preferred_element_type=jnp.float32)

        def sums_of(mine, other, their_mine, their_other):
            return jnp.concatenate([pair(mine, other), pair(their_other, their_mine)], axis=3)

        def across(total):
            for pairs in wider:
                total = total + send(total.astype(jnp.bfloat16), pairs).astype(jnp.float32)
            return total

        def term(total, mine, other, their_mine, their_other, far):
            swapped = jnp.transpose(total, (1, 0, 2, 3))
            t = ((2.0 * total - swapped) / (base - far[None, None, None, :])).astype(jnp.bfloat16)

            def product(ring, core):
                return jnp.einsum(
                    "ijab,jbp->iap", t, jnp.concatenate([ring, core], 1), preferred_element_type=jnp.float32
                )

            return product(mine, their_other), product(other, their_mine)

        def swap(mine, other):
            return send(mine, core), send(other, core)

        if in_pairs:
            sums, totals, sent = [], [], []
            for step in range(cycle_size):
                if step >= 2:
                    mine, totals[step - 1], sent[step - 2] = lax.optimization_barrier((mine, totals[step - 1], sent[step - 2]))
                if step >= 4:
                    other, sums[step - 3] = lax.optimization_barrier((other, sums[step - 3]))
                if step + 1 < cycle_size:
                    next_mine, next_other = send(mine, onward), send(other, onward)
                theirs = swap(mine, other) if step else (send(near_mine, core), apart_mine)
                totals.append(pair(jnp.concatenate([mine, theirs[1]], 1), jnp.concatenate([other, theirs[0]], 1)))
                if step >= 1:
                    totals[step], sent[step - 1] = lax.optimization_barrier((totals[step], sent[step - 1]))
                sent.append(across(totals[-1]))
                new = term(sent[-1], mine, other, *theirs, far[step])
                sums.append(new if step == 0 else (sums[-1][0] + new[0], sums[-1][1] + new[1]))
                mine, other = next_mine, next_other
            sum_mine, sum_other = sums[-1]
        else:

            def one_step(step, carry):
                mine, other, sum_mine, sum_other = carry
                mine, other = send(mine, onward), send(other, onward)
                theirs = swap(mine, other)
                new = term(
                    across(sums_of(mine, other, *theirs)),
                    mine,
                    other,
                    *theirs,
                    lax.dynamic_index_in_dim(far, step, 0, keepdims=False),
                )
                return mine, other, sum_mine + new[0], sum_other + new[1]

            theirs = swap(mine, other)
            first = term(across(sums_of(mine, other, *theirs)), mine, other, *theirs, far[0])
            sum_mine, sum_other = lax.fori_loop(1, cycle_size, one_step, (mine, other, *first))[2:]
        near_gamma, apart_gamma = sum_mine.astype(jnp.bfloat16), send(sum_other.astype(jnp.bfloat16), core)
        gamma = jnp.concatenate(
            [jnp.where(even, near_gamma, apart_gamma), jnp.where(even, apart_gamma, near_gamma)], axis=1
        ).reshape(occupied * tile_rows, width)

        if not in_pairs:
            lengths = lax.dynamic_index_in_dim(block_lengths, group, 0, keepdims=False)
            owners = lax.dynamic_index_in_dim(block_owner, group, 0, keepdims=False)
            starts = jnp.cumsum(lengths) - lengths
            match = owners[None, :] == jnp.arange(cycle_size, dtype=jnp.int32)[:, None]
            to_start = jnp.sum(jnp.where(match, starts[None, :], 0), axis=1)
            to_length = jnp.sum(jnp.where(match, lengths[None, :], 0), axis=1)
            slot = jnp.arange(capacity, dtype=jnp.int32)
            column = jnp.arange(width, dtype=jnp.int32)
            wanted = jnp.where(slot[None, :] < to_length[:, None], to_start[:, None] + slot[None, :], -1)
            marks = (wanted.reshape(-1, 1) == column[None, :]).astype(jnp.bfloat16)
            outgoing = jnp.einsum("sp,rp->sr", marks, gamma, preferred_element_type=jnp.float32)
            outgoing = outgoing.astype(jnp.bfloat16).reshape(cycle_size, capacity, occupied * tile_rows)
            incoming = lax.all_to_all(outgoing, "occ", split_axis=0, concat_axis=0, tiled=True)
            incoming = incoming.reshape(cycle_size, capacity, occupied, tile_rows)
            return jnp.transpose(incoming, (1, 2, 0, 3)).reshape(capacity, occupied, cycle_size * tile_rows)

        shape = (capacity, occupied, cycle_size * tile_rows)

        def after(array, other):
            return lax.optimization_barrier((array, other))[0]

        rises = sorted(range(1, heights), key=lambda rise: min(rise, heights - rise))
        landed = {}
        for at, rise in enumerate(rises):
            piece = pack(pack_table, gamma, rise, 0, capacity, occupied)
            if at >= 2:
                piece = after(piece, landed[rises[at - 2]])
            landed[rise] = send(piece, along_planes(rise))
        landed[0] = pack(pack_table, gamma, 0, 0, capacity, occupied)
        theirs = {rise: send(landed[rise], partner) for rise in [0] + rises[:-1]}
        gamma = after(gamma, theirs[0])
        more = {rise: pack(pack_table, gamma, rise, capacity, capacity, occupied) for rise in rises + [0]}
        joined = {rise: join(join_table, more[rise], send(more[rise], core), rise) for rise in rises}
        result = None
        for rise in [0] + rises[:-1]:
            result = place(place_table, [theirs[rise]], result, rise * members + 1, shape, tile_rows)
        result = place(place_table, [landed[0], more[0]], result, 0, shape, tile_rows)

        def rest(room, joined, place_table, landed, odd, result):
            lanes = {}
            for rise in rises:
                lane = lax.dynamic_slice_in_dim(joined[rise], odd * room, room, allow_negative_indices=False)
                lanes[rise] = send(lane, along_planes(rise))
            last = send(landed[rises[-1]], partner)
            for rise in rises:
                if rise == rises[-1]:
                    result = place(place_table, [last], result, rise * members + 1, shape, tile_rows)
                mine = [landed[rise], lanes[rise], send(lanes[rise], core)]
                result = place(place_table, mine, result, rise * members, shape, tile_rows)
            return result

        rests = [functools.partial(rest, room) for room in rooms]
        return lax.switch(which[0], rests, joined, place_table, landed, group % 2, result)

    placed = (P(None, "occ", "vir"), P(), P(), P(), P())
    return jax.shard_map(
        per_device,
        mesh=mesh,
        in_specs=placed,
        out_specs=P(("occ", "vir"), None, None),
        check_vma=False,
    )
```

```python
import functools
import math

import jax
import jax.numpy as jnp
from jax import lax
from jax.experimental import pallas as pl
from jax.experimental.pallas import tpu as pltpu
from jax.sharding import PartitionSpec as P

def grid_cycle(places):
    spans = [sorted({p[d] for p in places}) for d in range(len(places[0]))]
    order = sorted(range(len(spans)), key=lambda d: -len(spans[d]))
    grid = {}
    for index, p in enumerate(places):
        grid[tuple(spans[d].index(p[d]) for d in order)] = index
    sizes = [len(spans[d]) for d in order]

    def snake(dims):
        if not dims:
            return [()]
        inner, out = snake(dims[1:]), []
        for k in range(dims[0]):
            out += [(k,) + rest for rest in (inner if k % 2 == 0 else inner[::-1])]
        return out

    rest = snake(sizes[1:])
    walk = [(k,) + rest[0] for k in range(sizes[0])]
    for back, k in enumerate(reversed(range(sizes[0]))):
        line = rest[1:]
        walk += [(k,) + r for r in (line if back % 2 == 0 else line[::-1])]
    return [grid[w] for w in walk]


def pack_kernel(rise, base, table_ref, gamma_ref, out_ref):
    slots, occupied, tile_rows = out_ref.shape
    width = gamma_ref.shape[1]
    slot = base + pl.program_id(0) * slots + lax.broadcasted_iota(jnp.int32, (slots, width), 0)
    column = lax.broadcasted_iota(jnp.int32, (slots, width), 1)
    first, count = table_ref[rise, 0], table_ref[rise, 1]
    second, more = table_ref[rise, 2], table_ref[rise, 3]
    wanted = jnp.where(slot < count, first + slot, second + slot - count)
    marks = jnp.where((column == wanted) & (slot < count + more), 1.0, 0.0).astype(jnp.bfloat16)
    picked = lax.dot_general(marks, gamma_ref[...], (((1,), (1,)), ((), ())), preferred_element_type=jnp.float32)
    for i in range(occupied):
        out_ref[:, i, :] = picked[:, i * tile_rows : (i + 1) * tile_rows].astype(jnp.bfloat16)


def pack(table, gamma, rise, base, room, occupied):
    rows, width = gamma.shape
    steps = 2 if room % 32 == 0 and room > 256 else 1
    return pl.pallas_call(
        functools.partial(pack_kernel, rise, base),
        grid_spec=pltpu.PrefetchScalarGridSpec(
            num_scalar_prefetch=1,
            grid=(steps,),
            in_specs=[pl.BlockSpec((rows, width), lambda g, table: (0, 0))],
            out_specs=pl.BlockSpec((room // steps, occupied, rows // occupied), lambda g, table: (g, 0, 0)),
        ),
        out_shape=jax.ShapeDtypeStruct((room, occupied, rows // occupied), jnp.bfloat16),
        compiler_params=pltpu.CompilerParams(vmem_limit_bytes=40 << 20),
        cost_estimate=pl.CostEstimate(
            flops=2 * room * rows * width, bytes_accessed=2 * rows * (width + room), transcendentals=0
        ),
    )(table, gamma)


def copy_slots(out_ref, at, source_ref):
    few = math.gcd(source_ref.shape[0], 32)

    @pl.loop(0, source_ref.shape[0] // few)
    def _(k):
        out_ref[pl.ds(at + k * few, few)] = source_ref[pl.ds(k * few, few)]


def join_kernel(rise, table_ref, mine_ref, theirs_ref, out_ref):
    first = table_ref[rise, 0]

    @pl.when(table_ref[rise, 1] == 0)
    def _():
        copy_slots(out_ref, 0, mine_ref)
        copy_slots(out_ref, first, theirs_ref)

    @pl.when(table_ref[rise, 1] != 0)
    def _():
        copy_slots(out_ref, 0, theirs_ref)
        copy_slots(out_ref, first, mine_ref)


def join(table, mine, theirs, rise):
    slots, occupied, tile_rows = mine.shape
    return pl.pallas_call(
        functools.partial(join_kernel, rise),
        in_specs=[pl.BlockSpec(memory_space=pltpu.SMEM)] + [pl.BlockSpec(memory_space=pltpu.VMEM)] * 2,
        out_specs=pl.BlockSpec(memory_space=pltpu.VMEM),
        out_shape=jax.ShapeDtypeStruct((2 * slots, occupied, tile_rows), jnp.bfloat16),
        compiler_params=pltpu.CompilerParams(vmem_limit_bytes=40 << 20),
        cost_estimate=pl.CostEstimate(
            flops=slots, bytes_accessed=8 * slots * occupied * tile_rows, transcendentals=0
        ),
    )(table, mine, theirs)


def place_kernel(at, parts, table_ref, *refs):
    out_ref, seam_ref, later_ref = refs[-3:]
    slots = out_ref.shape[0]
    offset, length, skip, odd = [table_ref[at, k] for k in range(1, 5)]
    few = seam_ref.shape[0] // 2
    first_ref = refs[0]
    if parts == 2:
        copy_slots(later_ref, 0, refs[1])
    if parts == 3:
        lane = refs[1].shape[0]

        @pl.when(odd == 0)
        def _():
            copy_slots(later_ref, 0, refs[1])
            copy_slots(later_ref, lane, refs[2])

        @pl.when(odd != 0)
        def _():
            copy_slots(later_ref, 0, refs[2])
            copy_slots(later_ref, lane, refs[1])

    if parts > 1:
        seam_ref[pl.ds(0, few)] = first_ref[pl.ds(slots - few, few)]
        seam_ref[pl.ds(few, few)] = later_ref[pl.ds(skip, few)]

    def fill(k, source, start):
        @pl.when((k + 1) * few <= length)
        def _():
            out_ref[pl.ds(k * few, few)] = source[pl.ds(start, few)]

        @pl.when((k + 1) * few > length)
        def _():
            slot = k * few + lax.broadcasted_iota(jnp.int32, (few,) + out_ref.shape[1:], 0)
            block = source[pl.ds(start, few)].astype(jnp.float32)
            out_ref[pl.ds(k * few, few)] = jnp.where(slot < length, block, 0.0).astype(jnp.bfloat16)

    def some(k):
        if parts == 1:
            fill(k, first_ref, k * few)
            return
        start = offset + k * few
        last = slots - few

        @pl.when(start <= last)
        def _():
            fill(k, first_ref, start)

        @pl.when((start > last) & (start < slots))
        def _():
            fill(k, seam_ref, start - last)

        @pl.when(start >= slots)
        def _():
            fill(k, later_ref, skip + start - slots)

    @pl.loop(0, slots // few)
    def _(k):
        @pl.when(k * few >= length)
        def _():
            out_ref[pl.ds(k * few, few)] = jnp.zeros((few,) + out_ref.shape[1:], jnp.bfloat16)

        @pl.when(k * few < length)
        def _():
            some(k)


def place(table, pieces, result, at, shape, tile_rows):
    slots, occupied = shape[0], shape[1]
    whole = [] if result is None else [result]
    return pl.pallas_call(
        functools.partial(place_kernel, at, len(pieces)),
        grid_spec=pltpu.PrefetchScalarGridSpec(
            num_scalar_prefetch=1,
            grid=(1,),
            in_specs=[pl.BlockSpec(x.shape, lambda g, table: (0, 0, 0)) for x in pieces]
            + [pl.BlockSpec(memory_space=pl.ANY)] * len(whole),
            out_specs=pl.BlockSpec((slots, occupied, tile_rows), lambda g, table: (0, 0, table[at, 0])),
            scratch_shapes=[
                pltpu.VMEM((2 * math.gcd(slots, 32), occupied, tile_rows), jnp.bfloat16),
                pltpu.VMEM((2 * slots + 64 if len(pieces) > 1 else 8, occupied, tile_rows), jnp.bfloat16),
            ],
        ),
        out_shape=jax.ShapeDtypeStruct(shape, jnp.bfloat16),
        input_output_aliases={1 + len(pieces): 0} if whole else {},
        compiler_params=pltpu.CompilerParams(vmem_limit_bytes=40 << 20),
        cost_estimate=pl.CostEstimate(
            flops=slots * occupied * tile_rows,
            bytes_accessed=6 * slots * occupied * tile_rows,
            transcendentals=0,
        ),
    )(table, *pieces, *whole)


def setup_kernel(rooms, capacity, turns, at_ref, order_ref, lengths_ref, owners_ref, energy_ref, *outs):
    down_ref, up_ref, near_ref, pack_ref, place_ref, join_ref, which_ref = outs
    me, group = at_ref[0], at_ref[1]
    cycle_size = energy_ref.shape[0]
    heights = turns // 2
    groups, blocks = lengths_ref.shape
    near_ref[...] = energy_ref[pl.ds(me, 1), :]
    for step in range(cycle_size):
        down_ref[pl.ds(step, 1), :] = energy_ref[pl.ds(order_ref[me, step], 1), :]
        up_ref[pl.ds(step, 1), :] = energy_ref[pl.ds(order_ref[me, cycle_size + step], 1), :]
    targets, sources, levels = 2 * cycle_size, 2 * cycle_size + turns, 2 * cycle_size + 2 * turns
    found = []
    for turn in range(turns):
        owner = order_ref[me, targets + turn]
        start, length, so_far = jnp.int32(0), jnp.int32(0), jnp.int32(0)
        for k in range(blocks):
            hit = owners_ref[group, k] == owner
            start = jnp.where(hit, so_far, start)
            length = jnp.where(hit, lengths_ref[group, k], length)
            so_far = so_far + lengths_ref[group, k]
        pack_ref[turn // 2, 2 * (turn % 2)] = start
        pack_ref[turn // 2, 2 * (turn % 2) + 1] = length
        found.append(length)
    later = []
    for g in range(groups):
        held = [jnp.int32(0)] * heights
        for k in range(blocks):
            level = order_ref[owners_ref[g, k], levels]
            held = [h + jnp.where(level == at, lengths_ref[g, k], 0) for at, h in enumerate(held)]
        later.append([jnp.maximum(h - capacity, 0) for h in held])
    need = jnp.int32(0)
    for g in range(0, groups, 2):
        for one, two in zip(later[g], later[g + 1]):
            need = jnp.maximum(need, (one + two + 1) // 2)
    odd = group % 2
    my_level = order_ref[me, levels]
    for rise in range(heights):
        evens = jnp.int32(0)
        for g in range(0, groups, 2):
            for level in range(heights):
                here = (group - odd == g) & ((my_level + rise) % heights == level)
                evens = jnp.where(here, later[g][level], evens)
        join_ref[rise, 0] = evens
        join_ref[rise, 1] = odd
        if rise == 0:
            skip = jnp.where(odd == 0, 0, evens)
    for turn in range(turns):
        place_ref[turn, 0] = order_ref[me, sources + turn]
        place_ref[turn, 1] = found[0] if turn % 2 == 0 else jnp.int32(0)
        place_ref[turn, 2] = found[1]
        place_ref[turn, 3] = skip if turn >= 2 else jnp.int32(0)
        place_ref[turn, 4] = odd
    which = jnp.int32(0)
    for room in rooms[:-1]:
        which = which + jnp.where(need > room, 1, 0)
    which_ref[0] = which


def setup(at, order, lengths, owners, energy, rooms, capacity, turns):
    scalars, vectors = pl.BlockSpec(memory_space=pltpu.SMEM), pl.BlockSpec(memory_space=pltpu.VMEM)
    return pl.pallas_call(
        functools.partial(setup_kernel, rooms, capacity, turns),
        in_specs=[scalars] * 4 + [vectors],
        out_specs=[vectors] * 3 + [scalars] * 4,
        out_shape=[
            jax.ShapeDtypeStruct(energy.shape, jnp.float32),
            jax.ShapeDtypeStruct(energy.shape, jnp.float32),
            jax.ShapeDtypeStruct((1, energy.shape[1]), jnp.float32),
            jax.ShapeDtypeStruct((turns // 2, 4), jnp.int32),
            jax.ShapeDtypeStruct((turns, 5), jnp.int32),
            jax.ShapeDtypeStruct((turns // 2, 2), jnp.int32),
            jax.ShapeDtypeStruct((1,), jnp.int32),
        ],
    )(at, order, lengths, owners, energy)


def solution(mesh):
    cycle_size, groups = mesh.shape["occ"], mesh.shape["vir"]
    places = [tuple(row[0].coords) for row in mesh.devices.reshape(cycle_size, groups)]
    cycle = grid_cycle(places)
    position_of = [cycle.index(k) for k in range(cycle_size)]
    long_axis = max(range(3), key=lambda d: len({p[d] for p in places}))
    levels = sorted({p[long_axis] for p in places})
    planes = [[k for k in range(cycle_size) if places[k][long_axis] == level] for level in levels]
    heights, members = len(planes), len(planes[0])
    plane_of = [levels.index(p[long_axis]) for p in places]
    member_of = [planes[plane_of[k]].index(k) for k in range(cycle_size)]
    in_pairs = cycle_size <= 16 and members == 2

    def pairs_of(target):
        return [(k * groups + v, target(k, v) * groups + v) for k in range(cycle_size) for v in range(groups)]

    def along_planes(shift):
        return pairs_of(lambda k, v: planes[(plane_of[k] + shift) % heights][member_of[k]])

    def across_groups(bit):
        return [(k * groups + v, k * groups + (v ^ bit)) for k in range(cycle_size) for v in range(groups)]

    def send(array, pairs):
        return lax.ppermute(array, ("occ", "vir"), pairs)

    onward = pairs_of(lambda k, v: cycle[(position_of[k] + (1 if v % 2 == 0 else -1)) % cycle_size])
    partner = pairs_of(lambda k, v: planes[plane_of[k]][(member_of[k] + 1) % members])
    core = across_groups(1)
    wider = [across_groups(1 << bit) for bit in range(1, groups.bit_length() - 1)]

    def per_device(factors, occ_energy, vir_energy, block_lengths, block_owner):
        me, group = lax.axis_index("occ"), lax.axis_index("vir")
        occupied, tile_rows, width = factors.shape
        capacity = 8 * width // (3 * cycle_size)
        half = tile_rows // 2
        even = group % 2 == 0

        def of_me(table):
            return lax.dynamic_index_in_dim(
                jnp.array(table, jnp.int32), me, 0, keepdims=False, allow_negative_indices=False
            )

        low, high = factors[:, :half], factors[:, half:]
        near_mine, apart_mine = jnp.where(even, low, high), jnp.where(even, high, low)
        mine, other = near_mine, send(apart_mine, core)
        rows_mine, rows_other = mine, other

        tiles = vir_energy.reshape(cycle_size, tile_rows)
        if in_pairs:
            order = [
                [cycle[position_of[k] - step] for step in range(cycle_size)]
                + [cycle[(position_of[k] + step) % cycle_size] for step in range(cycle_size)]
                + [
                    planes[(plane_of[k] + rise) % heights][(member_of[k] + 1 - turn) % members]
                    for rise in range(heights)
                    for turn in range(members)
                ]
                + [
                    planes[(plane_of[k] - rise) % heights][(member_of[k] + turn) % members]
                    for rise in range(heights)
                    for turn in range(members)
                ]
                + [plane_of[k]]
                for k in range(cycle_size)
            ]
            grain = capacity // 16
            rooms = [grain * k for k in (1, 2, 3, 4, 5, 6, 7, 8, 10, 12, 14, 16)]
            other, tiles = lax.optimization_barrier((other, tiles))
            at = jnp.stack([me, group]).astype(jnp.int32)
            order = jnp.array(order, jnp.int32)
            down, up, own, pack_table, place_table, join_table, which = setup(
                at, order, block_lengths, block_owner, tiles, rooms, capacity, heights * members
            )
            own = own[0]
        else:
            in_cycle = jnp.stack([tiles[k] for k in cycle + cycle])
            up = lax.dynamic_slice_in_dim(in_cycle, of_me(position_of), cycle_size, allow_negative_indices=False)
            down = jnp.stack([up[-k] for k in range(cycle_size)])
            own = lax.dynamic_index_in_dim(tiles, me, 0, keepdims=False, allow_negative_indices=False)
        far_low, far_high = down[:, :half], up[:, half:]
        far = jnp.where(
            even, jnp.concatenate([far_low, far_high], 1), jnp.concatenate([far_high, far_low], 1)
        )
        near = jnp.where(even, own[:half], own[half:])
        base = (occ_energy[:, None] + occ_energy[None, :])[:, :, None, None] - near[None, None, :, None]

        def pair(first, second):
            one = jnp.einsum("iap,jbp->ijab", rows_mine, first, preferred_element_type=jnp.float32)
            return one + jnp.einsum("iap,jbp->ijab", rows_other, second, preferred_element_type=jnp.float32)

        def sums_of(mine, other, their_mine, their_other):
            return jnp.concatenate([pair(mine, other), pair(their_other, their_mine)], axis=3)

        def across(total):
            for pairs in wider:
                total = total + send(total.astype(jnp.bfloat16), pairs).astype(jnp.float32)
            return total

        def term(total, mine, other, their_mine, their_other, far):
            swapped = jnp.transpose(total, (1, 0, 2, 3))
            t = ((2.0 * total - swapped) / (base - far[None, None, None, :])).astype(jnp.bfloat16)

            def product(ring, core):
                return jnp.einsum(
                    "ijab,jbp->iap", t, jnp.concatenate([ring, core], 1), preferred_element_type=jnp.float32
                )

            return product(mine, their_other), product(other, their_mine)

        def swap(mine, other):
            return send(mine, core), send(other, core)

        if in_pairs:
            sums, totals, sent = [], [], []
            for step in range(cycle_size):
                if step >= 2:
                    mine, totals[step - 1], sent[step - 2] = lax.optimization_barrier((mine, totals[step - 1], sent[step - 2]))
                if step >= 4:
                    other, sums[step - 3] = lax.optimization_barrier((other, sums[step - 3]))
                if step + 1 < cycle_size:
                    next_mine, next_other = send(mine, onward), send(other, onward)
                theirs = swap(mine, other) if step else (send(near_mine, core), apart_mine)
                totals.append(pair(jnp.concatenate([mine, theirs[1]], 1), jnp.concatenate([other, theirs[0]], 1)))
                if step >= 1:
                    totals[step], sent[step - 1] = lax.optimization_barrier((totals[step], sent[step - 1]))
                sent.append(across(totals[-1]))
                new = term(sent[-1], mine, other, *theirs, far[step])
                sums.append(new if step == 0 else (sums[-1][0] + new[0], sums[-1][1] + new[1]))
                mine, other = next_mine, next_other
            sum_mine, sum_other = sums[-1]
        else:

            def one_step(step, carry):
                mine, other, sum_mine, sum_other = carry
                mine, other = send(mine, onward), send(other, onward)
                theirs = swap(mine, other)
                new = term(
                    across(sums_of(mine, other, *theirs)),
                    mine,
                    other,
                    *theirs,
                    lax.dynamic_index_in_dim(far, step, 0, keepdims=False),
                )
                return mine, other, sum_mine + new[0], sum_other + new[1]

            theirs = swap(mine, other)
            first = term(across(sums_of(mine, other, *theirs)), mine, other, *theirs, far[0])
            sum_mine, sum_other = lax.fori_loop(1, cycle_size, one_step, (mine, other, *first))[2:]
        near_gamma, apart_gamma = sum_mine.astype(jnp.bfloat16), send(sum_other.astype(jnp.bfloat16), core)
        gamma = jnp.concatenate(
            [jnp.where(even, near_gamma, apart_gamma), jnp.where(even, apart_gamma, near_gamma)], axis=1
        ).reshape(occupied * tile_rows, width)

        if not in_pairs:
            lengths = lax.dynamic_index_in_dim(block_lengths, group, 0, keepdims=False)
            owners = lax.dynamic_index_in_dim(block_owner, group, 0, keepdims=False)
            starts = jnp.cumsum(lengths) - lengths
            match = owners[None, :] == jnp.arange(cycle_size, dtype=jnp.int32)[:, None]
            to_start = jnp.sum(jnp.where(match, starts[None, :], 0), axis=1)
            to_length = jnp.sum(jnp.where(match, lengths[None, :], 0), axis=1)
            slot = jnp.arange(capacity, dtype=jnp.int32)
            column = jnp.arange(width, dtype=jnp.int32)
            wanted = jnp.where(slot[None, :] < to_length[:, None], to_start[:, None] + slot[None, :], -1)
            marks = (wanted.reshape(-1, 1) == column[None, :]).astype(jnp.bfloat16)
            outgoing = jnp.einsum("sp,rp->sr", marks, gamma, preferred_element_type=jnp.float32)
            outgoing = outgoing.astype(jnp.bfloat16).reshape(cycle_size, capacity, occupied * tile_rows)
            incoming = lax.all_to_all(outgoing, "occ", split_axis=0, concat_axis=0, tiled=True)
            incoming = incoming.reshape(cycle_size, capacity, occupied, tile_rows)
            return jnp.transpose(incoming, (1, 2, 0, 3)).reshape(capacity, occupied, cycle_size * tile_rows)

        shape = (capacity, occupied, cycle_size * tile_rows)

        def after(array, other):
            return lax.optimization_barrier((array, other))[0]

        rises = sorted(range(1, heights), key=lambda rise: min(rise, heights - rise))
        landed = {}
        for at, rise in enumerate(rises):
            piece = pack(pack_table, gamma, rise, 0, capacity, occupied)
            if at >= 2:
                piece = after(piece, landed[rises[at - 2]])
            landed[rise] = send(piece, along_planes(rise))
        landed[0] = pack(pack_table, gamma, 0, 0, capacity, occupied)
        theirs = {rise: send(landed[rise], partner) for rise in [0] + rises[:-1]}
        gamma = after(gamma, theirs[0])
        more = {rise: pack(pack_table, gamma, rise, capacity, capacity, occupied) for rise in rises + [0]}
        joined = {rise: join(join_table, more[rise], send(more[rise], core), rise) for rise in rises}
        result = None
        for rise in [0] + rises[:-1]:
            result = place(place_table, [theirs[rise]], result, rise * members + 1, shape, tile_rows)
        result = place(place_table, [landed[0], more[0]], result, 0, shape, tile_rows)

        def rest(room, joined, place_table, landed, odd, result):
            lanes = {}
            for rise in rises[::-1]:
                lane = lax.dynamic_slice_in_dim(joined[rise], odd * room, room, allow_negative_indices=False)
                lanes[rise] = send(lane, along_planes(rise))
            last = send(landed[rises[-1]], partner)
            for rise in rises[::-1]:
                if rise == rises[0]:
                    result = place(place_table, [last], result, rises[-1] * members + 1, shape, tile_rows)
                    lanes[rise], result = lax.optimization_barrier((lanes[rise], result))
                mine = [landed[rise], lanes[rise], send(lanes[rise], core)]
                result = place(place_table, mine, result, rise * members, shape, tile_rows)
            return result

        rests = [functools.partial(rest, room) for room in rooms]
        return lax.switch(which[0], rests, joined, place_table, landed, group % 2, result)

    placed = (P(None, "occ", "vir"), P(), P(), P(), P())
    return jax.shard_map(
        per_device,
        mesh=mesh,
        in_specs=placed,
        out_specs=P(("occ", "vir"), None, None),
        check_vma=False,
    )
```
